32 devices in a mesh: seq: 8 (over z, y), head: 4 (over x, core).
Axes of the slice: x: 2, y: 2, z: 4, core: 2. Of those that a mesh axis runs over, the one named last changes fastest.
Arguments:
- queries: bfloat16 [4096, 3584], P(('seq', 'head')), may hold values from -256 to 256
- rotated_key_rows: bfloat16 [4096, 512], P(('seq', 'head')), may hold values from -5 to 5
- value_matrix: bfloat16 [4096, 512], P(('seq', 'head')), may hold values from -6 to 6
- cotangent: bfloat16 [4096, 3584], P(('seq', 'head')), may hold values from -6 to 6
- tree_mask: int32 [32, 4], P('seq'), may hold values from 0 to 1, as said below
Outputs:
- attention: bfloat16 [4096, 3584], P(('seq', 'head'))
- query_grad: bfloat16 [4096, 3584], P(('seq', 'head'))
- key_gradient: bfloat16 [4096, 512], P(('seq', 'head'))
- value_gradient: bfloat16 [4096, 512], P(('seq', 'head'))
The draws below stay inside these ranges and needn't reach their ends.
Inputs may be any that keep to these rules, and one draw needn't show every extreme that they name: `tree_mask`: rows of the prompt's 4 blocks are 0. All blocks of one response share one row: 1 on its first r columns and 0 after, with r from 1 to 4; the first response reads all 4 prompt blocks.
All inputs are finite; a program needn't handle non-finite values.
Results may differ from the reference program's by a relative error of at most 0.034.
Values may be sent and summed in bfloat16 or wider, within the bound.
No kernel may reach another device: no remote copies, remote signals or barrier semaphores. Data moves between devices by JAX's collectives and lax.ppermute only.
A program may use at most 128 MiB of HBM per device.

```python
import jax
import jax.numpy as jnp
from jax import lax

QUERY_HEADS = 28
KEY_VALUE_HEADS = 4
HEAD_SIZE = 128
SEQUENCE_TOKENS = 512
MASK_BLOCK_SIZE = 128
TREE_TOKENS = 4096
NBLK = 32
PBLK = 4
QUERY_PER_KEY = 7
N_SEQ = 8


def drawn_pair(key):
    base = jax.random.fold_in(key, 17)
    query_key, random_key_seed = jax.random.split(base, 2)
    queries = jnp.clip(jax.random.normal(query_key, (TREE_TOKENS, QUERY_HEADS * HEAD_SIZE), jnp.float32), -4.0, 4.0)
    rotated_key_rows = jnp.clip(jax.random.normal(random_key_seed, (TREE_TOKENS, KEY_VALUE_HEADS * HEAD_SIZE), jnp.float32), -4.0, 4.0)
    return (queries, rotated_key_rows)


def draw_queries(key, part):
    return drawn_pair(key)[0].astype(jnp.bfloat16)


def draw_rotated_key_rows(key, part):
    return drawn_pair(key)[1].astype(jnp.bfloat16)


def draw_tree_mask(key, part):
    segments = NBLK // PBLK
    reach = jax.random.randint(jax.random.fold_in(key, 29), (segments,), 1, PBLK + 1)
    reach = jnp.where(jnp.arange(segments) == 1, PBLK, reach)
    block_segment = jnp.arange(NBLK) // PBLK
    columns = jnp.arange(PBLK)
    reads = (columns[None, :] < reach[block_segment][:, None]) & (block_segment[:, None] > 0)
    return reads.astype(jnp.int32)


def block_levels(stream_key, extent, shards, smallest, high):
    gain = 1.0
    for position, blocks in shards:
        draws = jax.random.uniform(jax.random.fold_in(jax.random.fold_in(stream_key, 6), position), (blocks,), jnp.float32, smallest / len(shards), high / len(shards))
        gain = gain * jnp.repeat(jnp.exp(draws), extent[position] // blocks).reshape((-1,) + (1,) * (len(extent) - 1 - position))
    return gain


def scatter_about(rng, shape, spread, most, pieces=(), held_as=jnp.bfloat16):
    gain = block_levels(rng, shape, pieces, -0.22, 0.18) if pieces else 1.0
    entries = jax.random.normal(rng, shape, jnp.float32) * spread * gain
    return jnp.minimum(jnp.maximum(entries, -most), most).astype(held_as)


def setup_inputs(seed: int = 0) -> dict:
    key_of = jax.random.split(jax.random.key(seed), 6)
    return {
        "queries": draw_queries(jax.random.fold_in(key_of[5], 71), 0),
        "rotated_key_rows": draw_rotated_key_rows(jax.random.fold_in(key_of[5], 71), 0),
        "value_matrix": scatter_about(key_of[2], (TREE_TOKENS, KEY_VALUE_HEADS * HEAD_SIZE), 1.0, 6.0, ((0, 32),)),
        "cotangent": scatter_about(key_of[3], (TREE_TOKENS, QUERY_HEADS * HEAD_SIZE), 1.0, 6.0, ((0, 32),)),
        "tree_mask": draw_tree_mask(jax.random.fold_in(key_of[5], 71), 0),
    }


def segment_terms(segment, queries, rotated_key_rows, value_matrix, cotangent, tree_mask):
    start_row = segment * SEQUENCE_TOKENS
    query_head_count = lax.dynamic_slice_in_dim(queries, start_row, SEQUENCE_TOKENS, 0).astype(jnp.float32).reshape(SEQUENCE_TOKENS, KEY_VALUE_HEADS, QUERY_PER_KEY, HEAD_SIZE)
    head_cotangents = lax.dynamic_slice_in_dim(cotangent, start_row, SEQUENCE_TOKENS, 0).astype(jnp.float32).reshape(SEQUENCE_TOKENS, KEY_VALUE_HEADS, QUERY_PER_KEY, HEAD_SIZE)
    response_keys = lax.dynamic_slice_in_dim(rotated_key_rows, start_row, SEQUENCE_TOKENS, 0)
    response_values = lax.dynamic_slice_in_dim(value_matrix, start_row, SEQUENCE_TOKENS, 0)
    block_keys = jnp.concatenate([rotated_key_rows[:SEQUENCE_TOKENS], response_keys], 0).astype(jnp.float32).reshape(2 * SEQUENCE_TOKENS, KEY_VALUE_HEADS, HEAD_SIZE)
    block_values = jnp.concatenate([value_matrix[:SEQUENCE_TOKENS], response_values], 0).astype(jnp.float32).reshape(2 * SEQUENCE_TOKENS, KEY_VALUE_HEADS, HEAD_SIZE)
    mask_rows = lax.dynamic_slice(tree_mask, (segment * PBLK, jnp.int32(0)), (PBLK, PBLK))
    token_mask = jnp.repeat(jnp.repeat(mask_rows, MASK_BLOCK_SIZE, axis=0), MASK_BLOCK_SIZE, axis=1)
    prompt_reads = (token_mask > 0) & (segment > 0)
    positions = jnp.arange(SEQUENCE_TOKENS, dtype=jnp.int32)
    causal = positions[None, :] <= positions[:, None]
    allowed = jnp.concatenate([prompt_reads, causal], 1)
    score_scale = HEAD_SIZE ** -0.5
    scores = jnp.einsum("tjgd,ujd->jgtu", query_head_count, block_keys) * score_scale
    scores = jnp.where(allowed, scores, jnp.float32(-1e30))
    row_max = jnp.max(scores, axis=-1, keepdims=True)
    weights = jnp.where(allowed, jnp.exp(scores - row_max), jnp.float32(0.0))
    softmax_probs = weights / jnp.sum(weights, axis=-1, keepdims=True)
    rounded_probs = softmax_probs.astype(jnp.bfloat16).astype(jnp.float32)
    attention = jnp.einsum("jgtu,ujd->tjgd", rounded_probs, block_values).astype(jnp.bfloat16)
    out_delta = jnp.sum(head_cotangents * attention.astype(jnp.float32), axis=-1)
    out_delta = jnp.transpose(out_delta, (1, 2, 0))[..., None]
    dprob = jnp.einsum("tjgd,ujd->jgtu", head_cotangents, block_values)
    dscore = (softmax_probs * (dprob - out_delta)).astype(jnp.bfloat16).astype(jnp.float32)
    query_grad = (jnp.einsum("jgtu,ujd->tjgd", dscore, block_keys) * score_scale).astype(jnp.bfloat16)
    key_terms = jnp.einsum("jgtu,tjgd->ujd", dscore, query_head_count) * score_scale
    value_terms = jnp.einsum("jgtu,tjgd->ujd", rounded_probs, head_cotangents)
    return (attention.reshape(SEQUENCE_TOKENS, QUERY_HEADS * HEAD_SIZE), query_grad.reshape(SEQUENCE_TOKENS, QUERY_HEADS * HEAD_SIZE),
            key_terms[:SEQUENCE_TOKENS], value_terms[:SEQUENCE_TOKENS], key_terms[SEQUENCE_TOKENS:], value_terms[SEQUENCE_TOKENS:])


def reference(queries, rotated_key_rows, value_matrix, cotangent, tree_mask):
    def one_segment(segment):
        return segment_terms(segment, queries, rotated_key_rows, value_matrix, cotangent, tree_mask)

    result_list = lax.map(one_segment, jnp.arange(N_SEQ, dtype=jnp.int32))
    attention = result_list[0].reshape(TREE_TOKENS, QUERY_HEADS * HEAD_SIZE)
    query_grad = result_list[1].reshape(TREE_TOKENS, QUERY_HEADS * HEAD_SIZE)
    prompt_key_rows = jnp.sum(result_list[2], axis=0)
    prompt_value_rows = jnp.sum(result_list[3], axis=0)
    key_gradient = result_list[4].at[0].add(prompt_key_rows).reshape(TREE_TOKENS, KEY_VALUE_HEADS * HEAD_SIZE).astype(jnp.bfloat16)
    value_gradient = result_list[5].at[0].add(prompt_value_rows).reshape(TREE_TOKENS, KEY_VALUE_HEADS * HEAD_SIZE).astype(jnp.bfloat16)
    return (attention, query_grad, key_gradient, value_gradient)
```

```python
import functools
import math

import jax
import jax.numpy as jnp
from jax import lax
from jax.experimental import pallas as pl
from jax.experimental.pallas import tpu as pltpu
from jax.sharding import PartitionSpec as P

QUERY_HEADS = 28
KEY_VALUE_HEADS = 4
HEAD_SIZE = 128
GROUP = QUERY_HEADS // KEY_VALUE_HEADS
WIDTH = GROUP * HEAD_SIZE
SCALE = HEAD_SIZE ** (-0.5)
EXP2_SCALE = SCALE * math.log2(math.e)
MASKED = -1e30
VMEM_BYTES = 24 * 1024 * 1024


def dot_nt(a, b):
    return lax.dot_general(a, b, (((1,), (1,)), ((), ())), preferred_element_type=jnp.float32)


def dot_nn(a, b):
    return lax.dot_general(a, b, (((1,), (0,)), ((), ())), preferred_element_type=jnp.float32)


def head_rows(mine, sibling, g):
    columns = slice(g * HEAD_SIZE, (g + 1) * HEAD_SIZE)
    return jnp.concatenate([mine[:, columns], sibling[:, columns]], axis=0)


def causal_mask(scores, rows, h):
    lane = lax.broadcasted_iota(jnp.int32, (rows, rows), 1)
    sub = lax.broadcasted_iota(jnp.int32, (rows, rows), 0)
    ahead = lane - sub
    out = []
    for b in range(scores.shape[0] // rows):
        line = []
        for a in range(2):
            offset = ((h ^ b) - (h ^ a)) * rows
            tile = scores[b * rows : (b + 1) * rows, a * rows : (a + 1) * rows]
            line.append(jnp.where(ahead >= offset, tile, MASKED))
        out.append(jnp.concatenate(line, axis=1))
    return jnp.concatenate(out, axis=0)


def prompt_mask(scores, rows, h, s, tree_ref):
    lane = lax.broadcasted_iota(jnp.int32, (1, 2 * rows), 1)
    out = []
    for b in range(scores.shape[0] // rows):
        reads = [jnp.logical_and(tree_ref[h ^ a, h ^ b] > 0, s > 0) for a in range(2)]
        bias = [jnp.where(r, jnp.float32(0.0), jnp.float32(MASKED)) for r in reads]
        row = jnp.where(lane < rows, bias[0], bias[1])
        out.append(scores[b * rows : (b + 1) * rows] + row)
    return jnp.concatenate(out, axis=0)


def stats_kernel(ids, tree, qm, qs, cm, cs, near, far, stats):
    h = ids[0]
    rows = qm.shape[0]
    keys = jnp.concatenate([near[:, :HEAD_SIZE], far[:, :HEAD_SIZE]], axis=0)
    values = jnp.concatenate([near[:, HEAD_SIZE:], far[:, HEAD_SIZE:]], axis=0)
    for g in range(GROUP):
        q = head_rows(qm, qs, g)
        ct = head_rows(cm, cs, g)
        scores = causal_mask(dot_nt(keys, q), rows, h)
        top = jnp.max(scores, axis=0, keepdims=True)
        e = jnp.exp2((scores - top) * EXP2_SCALE)
        dprob = dot_nt(values, ct)
        stats[g, 0:1, :] = top
        stats[g, 1:2, :] = jnp.sum(e, axis=0, keepdims=True)
        stats[g, 2:3, :] = jnp.sum(e * dprob, axis=0, keepdims=True)


def prompt_kernel(ids, tree, qm, qs, cm, cs, near, far, own, stats, att, dq, terms, key_sum, value_sum):
    h = ids[0]
    s = ids[1]
    rows = qm.shape[0]
    keys = jnp.concatenate([near[:, :HEAD_SIZE], far[:, :HEAD_SIZE]], axis=0)
    values = jnp.concatenate([near[:, HEAD_SIZE:], far[:, HEAD_SIZE:]], axis=0)
    keys_t = keys.T
    values_t = values.T
    for g in range(GROUP):
        q = head_rows(qm, qs, g)
        ct = head_rows(cm, cs, g)
        scores = prompt_mask(dot_nt(keys, q), rows, h, s, tree)
        own_top = own[g, 0:1, :]
        top = jnp.maximum(own_top, jnp.max(scores, axis=0, keepdims=True))
        e = jnp.exp2((scores - top) * EXP2_SCALE)
        keep = jnp.exp2((own_top - top) * EXP2_SCALE)
        dprob = dot_nt(values, ct)
        inverse = 1.0 / (own[g, 1:2, :] * keep + jnp.sum(e, axis=0, keepdims=True))
        delta = (own[g, 2:3, :] * keep + jnp.sum(e * dprob, axis=0, keepdims=True)) * inverse
        probs = e * inverse
        rounded = probs.astype(jnp.bfloat16)
        dscore = (probs * (dprob - delta)).astype(jnp.bfloat16)
        stats[g, 0:1, :] = top
        stats[g, 1:2, :] = inverse
        stats[g, 2:3, :] = delta
        value_term = dot_nn(rounded, ct)
        key_term = dot_nn(dscore, q)
        if g == 0:
            value_sum[...] = value_term
            key_sum[...] = key_term
        else:
            value_sum[...] += value_term
            key_sum[...] += key_term
        att[g] = dot_nn(values_t, rounded)
        dq[g] = dot_nn(keys_t, dscore)
    terms[:, :HEAD_SIZE] = (key_sum[...] * SCALE).astype(terms.dtype)
    terms[:, HEAD_SIZE:] = value_sum[...].astype(terms.dtype)


def own_kernel(
    ids, tree, qm, qs, cm, cs, near, far, stats, att_p, dq_p,
    att_m, att_s, dq_m, dq_s, terms_near, terms_far, key_sum, value_sum,
):
    h = ids[0]
    rows = qm.shape[0]
    keys = jnp.concatenate([near[:, :HEAD_SIZE], far[:, :HEAD_SIZE]], axis=0)
    values = jnp.concatenate([near[:, HEAD_SIZE:], far[:, HEAD_SIZE:]], axis=0)
    keys_t = keys.T
    values_t = values.T
    for g in range(GROUP):
        columns = slice(g * HEAD_SIZE, (g + 1) * HEAD_SIZE)
        q = head_rows(qm, qs, g)
        ct = head_rows(cm, cs, g)
        scores = causal_mask(dot_nt(keys, q), rows, h)
        probs = jnp.exp2((scores - stats[g, 0:1, :]) * EXP2_SCALE) * stats[g, 1:2, :]
        dprob = dot_nt(values, ct)
        rounded = probs.astype(jnp.bfloat16)
        dscore = (probs * (dprob - stats[g, 2:3, :])).astype(jnp.bfloat16)
        value_term = dot_nn(rounded, ct)
        key_term = dot_nn(dscore, q)
        if g == 0:
            value_sum[...] = value_term
            key_sum[...] = key_term
        else:
            value_sum[...] += value_term
            key_sum[...] += key_term
        att = (att_p[g] + dot_nn(values_t, rounded)).T.astype(jnp.bfloat16)
        dq = ((dq_p[g] + dot_nn(keys_t, dscore)) * SCALE).T.astype(jnp.bfloat16)
        att_m[:, columns] = att[:rows]
        att_s[:, columns] = att[rows:]
        dq_m[:, columns] = dq[:rows]
        dq_s[:, columns] = dq[rows:]
    half = terms_near.shape[0]
    for out, part in ((terms_near, slice(0, half)), (terms_far, slice(half, 2 * half))):
        out[:, :HEAD_SIZE] = (key_sum[part, :] * SCALE).astype(out.dtype)
        out[:, HEAD_SIZE:] = value_sum[part, :].astype(out.dtype)


def full(shape):
    return pl.BlockSpec(shape, lambda i, *refs: (0,) * len(shape))


def call(kernel, j, scalars, inputs, outs, scratch, products):
    specs = []
    for x, where in inputs:
        if where == "mine":
            specs.append(
                pl.BlockSpec((x.shape[0], WIDTH), lambda i, ids, tree: (0, 2 * (ids[0] & 1) + j))
            )
        elif where == "half":
            specs.append(pl.BlockSpec((x.shape[0], WIDTH), lambda i, ids, tree: (0, j)))
        else:
            specs.append(full(x.shape))
    rows = inputs[0][0].shape[0]
    flops = 2 * products * (2 * rows * GROUP) * (4 * rows) * HEAD_SIZE
    return pl.pallas_call(
        kernel,
        grid_spec=pltpu.PrefetchScalarGridSpec(
            num_scalar_prefetch=2,
            grid=(1,),
            in_specs=specs,
            out_specs=[full(o.shape) for o in outs],
            scratch_shapes=scratch,
        ),
        out_shape=outs,
        compiler_params=pltpu.CompilerParams(vmem_limit_bytes=VMEM_BYTES),
        cost_estimate=pl.CostEstimate(
            flops=flops, bytes_accessed=4 * 2 * rows * WIDTH * 2, transcendentals=0
        ),
    )(*scalars, *[x for x, _ in inputs])


def on_device(seq_count, head_count, queries, rotated_key_rows, value_matrix, cotangent, tree_mask):
    s = lax.axis_index("seq")
    h = lax.axis_index("head")
    rows = queries.shape[0]
    half_heads = KEY_VALUE_HEADS // 2
    half = half_heads * HEAD_SIZE
    core = h & 1
    pair = [(i, i ^ 1) for i in range(head_count)]
    cross = [(i, i ^ 2) for i in range(head_count)]
    scalars = (jnp.stack([h, s]).astype(jnp.int32), tree_mask)

    def columns(x, place, width):
        return lax.dynamic_slice_in_dim(x, place * width, width, 1)

    def chunk(place, j):
        return jnp.concatenate(
            [
                columns(rotated_key_rows, half_heads * place + j, HEAD_SIZE),
                columns(value_matrix, half_heads * place + j, HEAD_SIZE),
            ],
            axis=1,
        )

    near, far, prompt_near, prompt_far = [], [], [], []
    for j in range(half_heads):
        got = lax.ppermute(chunk(1 - core, j), "head", pair)
        near.append(jnp.concatenate([chunk(core, j), got], axis=0))
    for j in range(half_heads):
        held = near[j]
        step = seq_count // 2
        while step:
            sends = [(i, i + step) for i in range(0, seq_count, 2 * step)]
            got = lax.ppermute(held, "seq", sends)
            held = jnp.where(s % (2 * step) == step, got, held)
            step //= 2
        prompt_near.append(held)
        prompt_far.append(lax.ppermute(held, "head", cross))
    for j in range(half_heads):
        far.append(lax.ppermute(near[j], "head", cross))

    query_width = half_heads * WIDTH
    q_sib = lax.ppermute(columns(queries, 1 - core, query_width), "head", pair)
    c_sib = lax.ppermute(columns(cotangent, 1 - core, query_width), "head", pair)

    f32, bf16 = jnp.float32, jnp.bfloat16
    shape = jax.ShapeDtypeStruct
    sums = [pltpu.VMEM((4 * rows, HEAD_SIZE), f32)] * 2
    stats_shape = shape((GROUP, 8, 2 * rows), f32)
    part_shape = shape((GROUP, HEAD_SIZE, 2 * rows), f32)
    rows_shape = shape((rows, WIDTH), bf16)
    att_m, att_s, dq_m, dq_s, totals = [], [], [], [], []
    heads = [
        [(queries, "mine"), (q_sib, "half"), (cotangent, "mine"), (c_sib, "half")]
        for _ in range(half_heads)
    ]
    own = [
        call(
            stats_kernel, j, scalars, heads[j] + [(near[j], ""), (far[j], "")], [stats_shape], [], 2
        )[0]
        for j in range(half_heads)
    ]
    mids = [
        call(
            prompt_kernel,
            j,
            scalars,
            heads[j] + [(prompt_near[j], ""), (prompt_far[j], ""), (own[j], "")],
            [stats_shape, part_shape, part_shape, shape((4 * rows, 2 * HEAD_SIZE), bf16)],
            sums,
            6,
        )
        for j in range(half_heads)
    ]
    prompt_sums = []
    for j in range(half_heads):
        terms = mids[j][3]
        got = lax.ppermute(terms[2 * rows :], "head", cross)
        total = terms[: 2 * rows].astype(f32) + got.astype(f32)
        step = 1
        while step < seq_count:
            sends = [(i + step, i) for i in range(0, seq_count, 2 * step)]
            got = lax.ppermute(total.astype(bf16), "seq", sends)
            total = total + got.astype(f32)
            step *= 2
        prompt_sums.append(total)
    for j in range(half_heads):
        a_m, a_s, d_m, d_s, t_near, t_far = call(
            own_kernel,
            j,
            scalars,
            heads[j] + [(near[j], ""), (far[j], "")] + [(x, "") for x in mids[j][:3]],
            [rows_shape] * 4 + [shape((2 * rows, 2 * HEAD_SIZE), f32), shape((2 * rows, 2 * HEAD_SIZE), bf16)],
            sums,
            6,
        )
        att_m.append(a_m)
        att_s.append(a_s)
        dq_m.append(d_m)
        dq_s.append(d_s)
        got = lax.ppermute(t_far, "head", cross)
        totals.append(t_near + got.astype(f32))

    def both_halves(mine, theirs):
        mine, theirs = jnp.concatenate(mine, axis=1), jnp.concatenate(theirs, axis=1)
        return jnp.where(
            core == 0,
            jnp.concatenate([mine, theirs], axis=1),
            jnp.concatenate([theirs, mine], axis=1),
        )

    def swap(x):
        return lax.ppermute(x, "head", pair)

    attention = both_halves(att_m, [swap(x) for x in att_s])
    query_grad = both_halves(dq_m, [swap(x) for x in dq_s])
    mine, theirs = [], []
    for j in range(half_heads):
        total = totals[j] + jnp.where(s == 0, prompt_sums[j], jnp.float32(0.0))
        total = total.astype(bf16)
        mine.append(total[:rows])
        theirs.append(swap(total[rows:]))
    key_gradient = both_halves(
        [x[:, :HEAD_SIZE] for x in mine], [x[:, :HEAD_SIZE] for x in theirs]
    )
    value_gradient = both_halves(
        [x[:, HEAD_SIZE:] for x in mine], [x[:, HEAD_SIZE:] for x in theirs]
    )
    return (attention, query_grad, key_gradient, value_gradient)


def solution(mesh):
    spec = P(("seq", "head"), None)
    return jax.shard_map(
        functools.partial(on_device, mesh.shape["seq"], mesh.shape["head"]),
        mesh=mesh,
        in_specs=(spec, spec, spec, spec, P("seq", None)),
        out_specs=(spec, spec, spec, spec),
        check_vma=False,
    )
```

```python
import functools
import math

import jax
import jax.numpy as jnp
from jax import lax
from jax.experimental import pallas as pl
from jax.experimental.pallas import tpu as pltpu
from jax.sharding import PartitionSpec as P

QUERY_HEADS = 28
KEY_VALUE_HEADS = 4
HEAD_SIZE = 128
GROUP = QUERY_HEADS // KEY_VALUE_HEADS
WIDTH = GROUP * HEAD_SIZE
SCALE = HEAD_SIZE ** (-0.5)
EXP2_SCALE = SCALE * math.log2(math.e)
MASKED = -1e30
VMEM_BYTES = 24 * 1024 * 1024


def dot_nt(a, b):
    return lax.dot_general(a, b, (((1,), (1,)), ((), ())), preferred_element_type=jnp.float32)


def dot_nn(a, b):
    return lax.dot_general(a, b, (((1,), (0,)), ((), ())), preferred_element_type=jnp.float32)


def head_rows(mine, sibling, g):
    columns = slice(g * HEAD_SIZE, (g + 1) * HEAD_SIZE)
    return jnp.concatenate([mine[:, columns], sibling[:, columns]], axis=0)


def causal_mask(scores, rows, h):
    lane = lax.broadcasted_iota(jnp.int32, (rows, rows), 1)
    sub = lax.broadcasted_iota(jnp.int32, (rows, rows), 0)
    ahead = lane - sub
    out = []
    for b in range(scores.shape[0] // rows):
        line = []
        for a in range(2):
            offset = ((h ^ b) - (h ^ a)) * rows
            tile = scores[b * rows : (b + 1) * rows, a * rows : (a + 1) * rows]
            line.append(jnp.where(ahead >= offset, tile, MASKED))
        out.append(jnp.concatenate(line, axis=1))
    return jnp.concatenate(out, axis=0)


def prompt_mask(scores, rows, h, s, tree_ref):
    lane = lax.broadcasted_iota(jnp.int32, (1, 2 * rows), 1)
    out = []
    for b in range(scores.shape[0] // rows):
        reads = [jnp.logical_and(tree_ref[h ^ a, h ^ b] > 0, s > 0) for a in range(2)]
        bias = [jnp.where(r, jnp.float32(0.0), jnp.float32(MASKED)) for r in reads]
        row = jnp.where(lane < rows, bias[0], bias[1])
        out.append(scores[b * rows : (b + 1) * rows] + row)
    return jnp.concatenate(out, axis=0)


def stats_kernel(ids, tree, qm, qs, cm, cs, near, far, stats):
    h = ids[0]
    rows = qm.shape[0]
    keys = jnp.concatenate([near[0, :, :HEAD_SIZE], far[0, :, :HEAD_SIZE]], axis=0)
    values = jnp.concatenate([near[0, :, HEAD_SIZE:], far[0, :, HEAD_SIZE:]], axis=0)
    for g in range(GROUP):
        q = head_rows(qm, qs, g)
        ct = head_rows(cm, cs, g)
        scores = causal_mask(dot_nt(keys, q), rows, h)
        top = jnp.max(scores, axis=0, keepdims=True)
        e = jnp.exp2((scores - top) * EXP2_SCALE)
        dprob = dot_nt(values, ct)
        stats[0, g, 0:1, :] = top
        stats[0, g, 1:2, :] = jnp.sum(e, axis=0, keepdims=True)
        stats[0, g, 2:3, :] = jnp.sum(e * dprob, axis=0, keepdims=True)


def prompt_kernel(ids, tree, qm, qs, cm, cs, near, far, own, stats, att, dq, terms, key_sum, value_sum):
    h = ids[0]
    s = ids[1]
    rows = qm.shape[0]
    keys = jnp.concatenate([near[0, :, :HEAD_SIZE], far[0, :, :HEAD_SIZE]], axis=0)
    values = jnp.concatenate([near[0, :, HEAD_SIZE:], far[0, :, HEAD_SIZE:]], axis=0)
    keys_t = keys.T
    values_t = values.T
    for g in range(GROUP):
        q = head_rows(qm, qs, g)
        ct = head_rows(cm, cs, g)
        scores = prompt_mask(dot_nt(keys, q), rows, h, s, tree)
        own_top = own[0, g, 0:1, :]
        top = jnp.maximum(own_top, jnp.max(scores, axis=0, keepdims=True))
        e = jnp.exp2((scores - top) * EXP2_SCALE)
        keep = jnp.exp2((own_top - top) * EXP2_SCALE)
        dprob = dot_nt(values, ct)
        inverse = 1.0 / (own[0, g, 1:2, :] * keep + jnp.sum(e, axis=0, keepdims=True))
        delta = (own[0, g, 2:3, :] * keep + jnp.sum(e * dprob, axis=0, keepdims=True)) * inverse
        probs = e * inverse
        rounded = probs.astype(jnp.bfloat16)
        dscore = (probs * (dprob - delta)).astype(jnp.bfloat16)
        stats[0, g, 0:1, :] = top
        stats[0, g, 1:2, :] = inverse
        stats[0, g, 2:3, :] = delta
        value_term = dot_nn(rounded, ct)
        key_term = dot_nn(dscore, q)
        if g == 0:
            value_sum[...] = value_term
            key_sum[...] = key_term
        else:
            value_sum[...] += value_term
            key_sum[...] += key_term
        att[0, g] = dot_nn(values_t, rounded)
        dq[0, g] = dot_nn(keys_t, dscore)
    terms[0, :, :HEAD_SIZE] = (key_sum[...] * SCALE).astype(terms.dtype)
    terms[0, :, HEAD_SIZE:] = value_sum[...].astype(terms.dtype)


def own_kernel(
    ids, tree, qm, qs, cm, cs, near, far, stats, att_p, dq_p,
    att_m, att_s, dq_m, dq_s, terms_near, terms_far, key_sum, value_sum,
):
    h = ids[0]
    rows = qm.shape[0]
    keys = jnp.concatenate([near[0, :, :HEAD_SIZE], far[0, :, :HEAD_SIZE]], axis=0)
    values = jnp.concatenate([near[0, :, HEAD_SIZE:], far[0, :, HEAD_SIZE:]], axis=0)
    keys_t = keys.T
    values_t = values.T
    for g in range(GROUP):
        columns = slice(g * HEAD_SIZE, (g + 1) * HEAD_SIZE)
        q = head_rows(qm, qs, g)
        ct = head_rows(cm, cs, g)
        scores = causal_mask(dot_nt(keys, q), rows, h)
        probs = jnp.exp2((scores - stats[0, g, 0:1, :]) * EXP2_SCALE) * stats[0, g, 1:2, :]
        dprob = dot_nt(values, ct)
        rounded = probs.astype(jnp.bfloat16)
        dscore = (probs * (dprob - stats[0, g, 2:3, :])).astype(jnp.bfloat16)
        value_term = dot_nn(rounded, ct)
        key_term = dot_nn(dscore, q)
        if g == 0:
            value_sum[...] = value_term
            key_sum[...] = key_term
        else:
            value_sum[...] += value_term
            key_sum[...] += key_term
        att = (att_p[0, g] + dot_nn(values_t, rounded)).T.astype(jnp.bfloat16)
        dq = ((dq_p[0, g] + dot_nn(keys_t, dscore)) * SCALE).T.astype(jnp.bfloat16)
        att_m[:, columns] = att[:rows]
        att_s[:, columns] = att[rows:]
        dq_m[:, columns] = dq[:rows]
        dq_s[:, columns] = dq[rows:]
    half = terms_near.shape[1]
    for out, part in ((terms_near, slice(0, half)), (terms_far, slice(half, 2 * half))):
        out[0, :, :HEAD_SIZE] = (key_sum[part, :] * SCALE).astype(out.dtype)
        out[0, :, HEAD_SIZE:] = value_sum[part, :].astype(out.dtype)


def per_head(shape):
    return pl.BlockSpec((1, *shape[1:]), lambda j, *refs: (j,) + (0,) * (len(shape) - 1))


def at_head(j, shape):
    return pl.BlockSpec((1, *shape[1:]), lambda i, *refs: (j,) + (0,) * (len(shape) - 1))


def full(shape):
    return pl.BlockSpec(shape, lambda i, *refs: (0,) * len(shape))


def call(kernel, j, scalars, heads, inputs, outs, scratch, products):
    queries, q_sib, cotangent, c_sib = heads
    rows = queries.shape[0]
    steps = q_sib.shape[1] // WIDTH
    mine = pl.BlockSpec(
        (rows, WIDTH), lambda i, ids, tree: (0, steps * (ids[0] & 1) + (i if j is None else j))
    )
    sib = pl.BlockSpec((rows, WIDTH), lambda i, *refs: (0, i if j is None else j))
    specs = [mine, sib, mine, sib]
    for x, per in inputs:
        if not per:
            specs.append(full(x.shape))
        elif j is None:
            specs.append(per_head(x.shape))
        else:
            specs.append(at_head(j, x.shape))
    out_specs = []
    for o in outs:
        if len(o.shape) == 2:
            out_specs.append(pl.BlockSpec((rows, WIDTH), lambda i, *refs: (0, i)))
        elif j is None:
            out_specs.append(per_head(o.shape))
        else:
            out_specs.append(full(o.shape))
    count = steps if j is None else 1
    flops = count * 2 * products * (2 * rows * GROUP) * (4 * rows) * HEAD_SIZE
    return pl.pallas_call(
        kernel,
        grid_spec=pltpu.PrefetchScalarGridSpec(
            num_scalar_prefetch=2,
            grid=(count,),
            in_specs=specs,
            out_specs=out_specs,
            scratch_shapes=scratch,
        ),
        out_shape=outs,
        compiler_params=pltpu.CompilerParams(vmem_limit_bytes=VMEM_BYTES),
        cost_estimate=pl.CostEstimate(
            flops=flops, bytes_accessed=count * 4 * 2 * rows * WIDTH * 2, transcendentals=0
        ),
    )(*scalars, *heads, *[x for x, _ in inputs])


def on_device(seq_count, head_count, queries, rotated_key_rows, value_matrix, cotangent, tree_mask):
    s = lax.axis_index("seq")
    h = lax.axis_index("head")
    rows = queries.shape[0]
    heads = KEY_VALUE_HEADS // 2
    core = h & 1
    pair = [(i, i ^ 1) for i in range(head_count)]
    cross = [(i, i ^ 2) for i in range(head_count)]
    scalars = (jnp.stack([h, s]).astype(jnp.int32), tree_mask)
    f32, bf16 = jnp.float32, jnp.bfloat16

    def columns(x, place, width):
        return lax.dynamic_slice_in_dim(x, place * width, width, 1)

    def half(place):
        k = columns(rotated_key_rows, place, heads * HEAD_SIZE).reshape(rows, heads, 1, HEAD_SIZE)
        v = columns(value_matrix, place, heads * HEAD_SIZE).reshape(rows, heads, 1, HEAD_SIZE)
        kv = jnp.concatenate([k, v], axis=2).reshape(rows, heads, 2 * HEAD_SIZE)
        return jnp.transpose(kv, (1, 0, 2))

    near = jnp.concatenate([half(core), lax.ppermute(half(1 - core), "head", pair)], axis=1)
    held, hops = near, []
    step = seq_count // 2
    while step:
        sends = [(i, i + step) for i in range(0, seq_count, 2 * step)]
        got = lax.ppermute(held, "seq", sends)
        held = jnp.where(s % (2 * step) == step, got, held)
        hops.append(held)
        step //= 2
    prompt_near = held
    prompt_far = [lax.ppermute(held[j : j + 1], "head", cross) for j in range(heads)]

    _, near_later = lax.optimization_barrier((hops[0], near))
    far = lax.ppermute(near_later, "head", cross)
    _, q_in, c_in = lax.optimization_barrier((hops[0], queries, cotangent))
    q_sib = lax.ppermute(columns(q_in, 1 - core, heads * WIDTH), "head", pair)
    c_sib = lax.ppermute(columns(c_in, 1 - core, heads * WIDTH), "head", pair)
    work = (queries, q_sib, cotangent, c_sib)

    shape = jax.ShapeDtypeStruct
    sums = [pltpu.VMEM((4 * rows, HEAD_SIZE), f32)] * 2

    def stats_shape(n):
        return shape((n, GROUP, 8, 2 * rows), f32)

    def part_shape(n):
        return shape((n, GROUP, HEAD_SIZE, 2 * rows), f32)

    own = call(
        stats_kernel, None, scalars, work, [(near, 1), (far, 1)], [stats_shape(heads)], [], 2
    )[0]
    mids, prompt_sums = [], []
    for j in range(heads):
        mid = call(
            prompt_kernel,
            j,
            scalars,
            work,
            [(prompt_near, 1), (prompt_far[j], 0), (own, 1)],
            [
                stats_shape(1),
                part_shape(1),
                part_shape(1),
                shape((1, 4 * rows, 2 * HEAD_SIZE), bf16),
            ],
            sums,
            6,
        )
        got = lax.ppermute(mid[3][0, 2 * rows :], "head", cross)
        mids.append(mid[:3])
        prompt_sums.append(mid[3][0, : 2 * rows].astype(f32) + got.astype(f32))
    total = jnp.stack(prompt_sums)
    step = 1
    while step < seq_count:
        sends = [(i + step, i) for i in range(0, seq_count, 2 * step)]
        total = total + lax.ppermute(total.astype(bf16), "seq", sends).astype(f32)
        step *= 2

    stats, att_p, dq_p = [jnp.concatenate(x, axis=0) for x in zip(*mids)]
    rows_shape = shape((rows, heads * WIDTH), bf16)
    att_m, att_s, dq_m, dq_s, t_near, t_far = call(
        own_kernel,
        None,
        scalars,
        work,
        [(x, 1) for x in (near, far, stats, att_p, dq_p)],
        [rows_shape] * 4
        + [
            shape((heads, 2 * rows, 2 * HEAD_SIZE), f32),
            shape((heads, 2 * rows, 2 * HEAD_SIZE), bf16),
        ],
        sums,
        6,
    )
    own_sums = t_near + lax.ppermute(t_far, "head", cross).astype(f32)

    def both_halves(mine, theirs):
        return jnp.where(
            core == 0,
            jnp.concatenate([mine, theirs], axis=1),
            jnp.concatenate([theirs, mine], axis=1),
        )

    attention = both_halves(att_m, lax.ppermute(att_s, "head", pair))
    query_grad = both_halves(dq_m, lax.ppermute(dq_s, "head", pair))
    total = (own_sums + jnp.where(s == 0, total, jnp.float32(0.0))).astype(bf16)
    mine, theirs = total[:, :rows], lax.ppermute(total[:, rows:], "head", pair)

    def gradient(part):
        return both_halves(
            jnp.concatenate([mine[j, :, part] for j in range(heads)], axis=1),
            jnp.concatenate([theirs[j, :, part] for j in range(heads)], axis=1),
        )

    return (
        attention,
        query_grad,
        gradient(slice(0, HEAD_SIZE)),
        gradient(slice(HEAD_SIZE, 2 * HEAD_SIZE)),
    )


def solution(mesh):
    spec = P(("seq", "head"), None)
    return jax.shard_map(
        functools.partial(on_device, mesh.shape["seq"], mesh.shape["head"]),
        mesh=mesh,
        in_specs=(spec, spec, spec, spec, P("seq", None)),
        out_specs=(spec, spec, spec, spec),
        check_vma=False,
    )
```

```python
import functools
import math

import jax
import jax.numpy as jnp
from jax import lax
from jax.experimental import pallas as pl
from jax.experimental.pallas import tpu as pltpu
from jax.sharding import PartitionSpec as P

QUERY_HEADS = 28
KEY_VALUE_HEADS = 4
HEAD_SIZE = 128
GROUP = QUERY_HEADS // KEY_VALUE_HEADS
WIDTH = GROUP * HEAD_SIZE
HEADS = KEY_VALUE_HEADS // 2
SCALE = HEAD_SIZE ** (-0.5)
EXP2_SCALE = SCALE * math.log2(math.e)
MASKED = -1e30
VMEM_BYTES = 16 * 1024 * 1024


def dot_nt(a, b):
    return lax.dot_general(a, b, (((1,), (1,)), ((), ())), preferred_element_type=jnp.float32)


def dot_nn(a, b):
    return lax.dot_general(a, b, (((1,), (0,)), ((), ())), preferred_element_type=jnp.float32)


def head_rows(mine, sibling, g):
    columns = slice(g * HEAD_SIZE, (g + 1) * HEAD_SIZE)
    return jnp.concatenate([mine[:, columns], sibling[:, columns]], axis=0)


def causal_mask(scores, places, rows, ids, tree):
    h = ids[0]
    lane = lax.broadcasted_iota(jnp.int32, (rows, rows), 1)
    sub = lax.broadcasted_iota(jnp.int32, (rows, rows), 0)
    ahead = lane - sub
    out = []
    for i, b in enumerate(places):
        line = []
        for a in range(2):
            offset = ((h ^ b) - (h ^ a)) * rows
            tile = scores[i * rows : (i + 1) * rows, a * rows : (a + 1) * rows]
            line.append(jnp.where(ahead >= offset, tile, MASKED))
        out.append(jnp.concatenate(line, axis=1))
    return jnp.concatenate(out, axis=0)


def prompt_mask(scores, places, rows, ids, tree):
    h, s = ids[0], ids[1]
    lane = lax.broadcasted_iota(jnp.int32, (1, 2 * rows), 1)
    out = []
    for i, b in enumerate(places):
        reads = [jnp.logical_and(tree[h ^ a, h ^ b] > 0, s > 0) for a in range(2)]
        bias = [jnp.where(r, jnp.float32(0.0), jnp.float32(MASKED)) for r in reads]
        row = jnp.where(lane < rows, bias[0], bias[1])
        out.append(scores[i * rows : (i + 1) * rows] + row)
    return jnp.concatenate(out, axis=0)


def keys_values(blocks):
    keys = jnp.concatenate([b[:, :HEAD_SIZE] for b in blocks], axis=0)
    values = jnp.concatenate([b[:, HEAD_SIZE:] for b in blocks], axis=0)
    return keys, values


def scores_of(segments, q, rows, ids, tree):
    parts = [mask(dot_nt(keys, q), places, rows, ids, tree) for mask, places, keys, _ in segments]
    return parts[0] if len(parts) == 1 else jnp.concatenate(parts, axis=0)


def dprob_of(segments, ct):
    parts = [dot_nt(values, ct) for _, _, _, values in segments]
    return parts[0] if len(parts) == 1 else jnp.concatenate(parts, axis=0)


def load(layout, refs):
    segments = []
    for mask, places in layout:
        segments.append((mask, places, *keys_values(refs[: len(places)])))
        refs = refs[len(places) :]
    return segments, refs


def stats_kernel(layout, ids, tree, qm, qs, cm, cs, *refs):
    segments, refs = load(layout, refs)
    stats = refs[-1]
    rows = qm.shape[0]
    for g in range(GROUP):
        q = head_rows(qm, qs, g)
        ct = head_rows(cm, cs, g)
        scores = scores_of(segments, q, rows, ids, tree)
        top = jnp.max(scores, axis=0, keepdims=True)
        e = jnp.exp2((scores - top) * EXP2_SCALE)
        stats[0, g, 0:1, :] = top
        stats[0, g, 1:2, :] = jnp.sum(e, axis=0, keepdims=True)
        stats[0, g, 2:3, :] = jnp.sum(e * dprob_of(segments, ct), axis=0, keepdims=True)


def add_terms(g, key_sum, value_sum, rounded, dscore, ct, q):
    value_term = dot_nn(rounded, ct)
    key_term = dot_nn(dscore, q)
    if g == 0:
        value_sum[...] = value_term
        key_sum[...] = key_term
    else:
        value_sum[...] += value_term
        key_sum[...] += key_term


def put_terms(out, part, key_sum, value_sum):
    out[:, :HEAD_SIZE] = (key_sum[part, :] * SCALE).astype(out.dtype)
    out[:, HEAD_SIZE:] = value_sum[part, :].astype(out.dtype)


def last_keys_kernel(layout, ids, tree, qm, qs, cm, cs, *refs):
    segments, refs = load(layout, refs)
    old, stats, terms, key_sum, value_sum = refs
    rows = qm.shape[0]
    for g in range(GROUP):
        q = head_rows(qm, qs, g)
        ct = head_rows(cm, cs, g)
        scores = scores_of(segments, q, rows, ids, tree)
        old_top = old[0, g, 0:1, :]
        top = jnp.maximum(jnp.max(scores, axis=0, keepdims=True), old_top)
        keep = jnp.exp2((old_top - top) * EXP2_SCALE)
        e = jnp.exp2((scores - top) * EXP2_SCALE)
        dprob = dprob_of(segments, ct)
        inverse = 1.0 / (jnp.sum(e, axis=0, keepdims=True) + old[0, g, 1:2, :] * keep)
        delta = jnp.sum(e * dprob, axis=0, keepdims=True) + old[0, g, 2:3, :] * keep
        delta = delta * inverse
        probs = e * inverse
        dscore = (probs * (dprob - delta)).astype(jnp.bfloat16)
        add_terms(g, key_sum, value_sum, probs.astype(jnp.bfloat16), dscore, ct, q)
        stats[0, g, 0:1, :] = top
        stats[0, g, 1:2, :] = inverse
        stats[0, g, 2:3, :] = delta
    put_terms(terms, slice(None), key_sum, value_sum)


def probs_dscore(segments, stats, g, q, ct, rows, ids, tree):
    scores = scores_of(segments, q, rows, ids, tree)
    probs = jnp.exp2((scores - stats[0, g, 0:1, :]) * EXP2_SCALE) * stats[0, g, 1:2, :]
    dscore = probs * (dprob_of(segments, ct) - stats[0, g, 2:3, :])
    return probs.astype(jnp.bfloat16), dscore.astype(jnp.bfloat16)


def terms_kernel(layout, ids, tree, qm, qs, cm, cs, *refs):
    segments, refs = load(layout, refs)
    stats, terms, key_sum, value_sum = refs
    for g in range(GROUP):
        q = head_rows(qm, qs, g)
        ct = head_rows(cm, cs, g)
        rounded, dscore = probs_dscore(segments, stats, g, q, ct, qm.shape[0], ids, tree)
        add_terms(g, key_sum, value_sum, rounded, dscore, ct, q)
    put_terms(terms, slice(None), key_sum, value_sum)


def rows_kernel(layout, ids, tree, qm, qs, cm, cs, *refs):
    segments, refs = load(layout, refs)
    stats, _, att_m, att_s, dq_m, dq_s, near, far, token, key_sum, value_sum = refs
    token[...] = jnp.zeros_like(token)
    rows = qm.shape[0]
    own = segments[0][2].shape[0]
    keys_t = jnp.concatenate([keys for _, _, keys, _ in segments], axis=0).T
    values_t = jnp.concatenate([values for _, _, _, values in segments], axis=0).T
    for g in range(GROUP):
        columns = slice(g * HEAD_SIZE, (g + 1) * HEAD_SIZE)
        q = head_rows(qm, qs, g)
        ct = head_rows(cm, cs, g)
        rounded, dscore = probs_dscore(segments, stats, g, q, ct, rows, ids, tree)
        add_terms(g, key_sum, value_sum, rounded[:own], dscore[:own], ct, q)
        att = dot_nn(values_t, rounded).T.astype(jnp.bfloat16)
        dq = (dot_nn(keys_t, dscore) * SCALE).T.astype(jnp.bfloat16)
        att_m[:, columns] = att[:rows]
        att_s[:, columns] = att[rows:]
        dq_m[:, columns] = dq[:rows]
        dq_s[:, columns] = dq[rows:]
    half = near.shape[0]
    put_terms(near, slice(0, half), key_sum, value_sum)
    put_terms(far, slice(half, 2 * half), key_sum, value_sum)


def call(kernel, layout, heads, scalars, work, blocks, inputs, outs, scratch, products, tie=None):
    rows = work[0].shape[0]
    first, count = heads
    mine = pl.BlockSpec((rows, WIDTH), lambda i, ids, tree: (0, HEADS * (ids[0] & 1) + i + first))

    def spec(shape, base):
        if len(shape) == 2:
            return pl.BlockSpec((shape[0], shape[1] // (HEADS if base is not None else count)), lambda i, *refs: (0, i + (base or 0)))
        return pl.BlockSpec((1, *shape[1:]), lambda i, *refs: (i + (base or 0),) + (0,) * (len(shape) - 1))

    sib = spec((rows, HEADS * WIDTH), first)
    specs = [mine, sib, mine, sib] + [spec(x.shape, first) for x in (*blocks, *inputs)]
    operands = [*scalars, *work, *blocks, *inputs]
    out_specs = [spec(o.shape, None) for o in outs]
    if tie is not None:
        operands.append(tie)
        specs.append(pl.BlockSpec((16, HEAD_SIZE), lambda i, *refs: (0, 0)))
        outs = [*outs, jax.ShapeDtypeStruct(tie.shape, tie.dtype)]
        out_specs.append(pl.BlockSpec(tie.shape, lambda i, *refs: (0, 0)))
    flops = count * 2 * products * (2 * rows * GROUP) * (len(blocks) * rows) * HEAD_SIZE
    return pl.pallas_call(
        functools.partial(kernel, layout),
        grid_spec=pltpu.PrefetchScalarGridSpec(
            num_scalar_prefetch=2,
            grid=(count,),
            in_specs=specs,
            out_specs=out_specs,
            scratch_shapes=scratch,
        ),
        out_shape=outs,
        compiler_params=pltpu.CompilerParams(vmem_limit_bytes=VMEM_BYTES),
        cost_estimate=pl.CostEstimate(
            flops=flops, bytes_accessed=count * 4 * 2 * rows * WIDTH * 2, transcendentals=0
        ),
    )(*operands)


def after(x, *tokens):
    return lax.optimization_barrier((x, *tokens))[0]


def on_device(seq_count, head_count, queries, rotated_key_rows, value_matrix, cotangent, tree_mask):
    s = lax.axis_index("seq")
    h = lax.axis_index("head")
    rows = queries.shape[0]
    core = h & 1
    scalars = (jnp.stack([h, s]).astype(jnp.int32), tree_mask)
    f32, bf16 = jnp.float32, jnp.bfloat16
    shape = jax.ShapeDtypeStruct

    def send(x, mask):
        return lax.ppermute(x, "head", [(i, i ^ mask) for i in range(head_count)])

    def columns(x, place, width):
        return lax.dynamic_slice_in_dim(x, place * width, width, 1)

    def half(kv, place):
        k, v = [columns(x, place, HEADS * HEAD_SIZE) for x in kv]
        parts = []
        for j in range(HEADS):
            part = slice(j * HEAD_SIZE, (j + 1) * HEAD_SIZE)
            parts += [k[:, part], v[:, part]]
        return jnp.concatenate(parts, axis=1)

    def gathered(kv, place):
        mine, other = half(kv, place), half(kv, 1 - place)
        return [mine, send(other, 1), send(mine, 2), send(other, 3)]

    hops = [1]
    step = seq_count // 2
    while step > 1:
        hops.append(step)
        step //= 2
    held = (rotated_key_rows, value_matrix)
    for hop, step in enumerate(hops):
        reached = seq_count if hop == 0 else 2 * step
        sends = [(i, i + step) for i in range(0, seq_count, reached)]
        if hop:
            sends += [(i + 1, i + 1 + step) for i, _ in sends]
            place = s - s % 2
            got = lax.ppermute(held, "seq", sends)
        else:
            place = s
            got = jnp.concatenate([lax.ppermute(x, "seq", sends) for x in held], axis=1)
            held = jnp.concatenate(held, axis=1)
        held = jnp.where(place % reached == step, got, held)
        if hop == 0:
            side = after(core, held[:16, :HEAD_SIZE])
            own_blocks = gathered((rotated_key_rows, value_matrix), side)
            q_sib = send(columns(queries, 1 - side, HEADS * WIDTH), 1)
            c_sib = send(columns(cotangent, 1 - side, HEADS * WIDTH), 1)
            work = (queries, q_sib, cotangent, c_sib)
    width = KEY_VALUE_HEADS * HEAD_SIZE
    prompt = (held[:, :width], held[:, width:])
    prompt_blocks = gathered(prompt, core)

    near, far = (0, 1), (2, 3)
    own_all = (causal_mask, near + far)
    every, one = (0, HEADS), 1

    def stats_shape():
        return shape((HEADS, GROUP, 8, 2 * rows), f32)

    def terms_shape(count, dtype):
        return shape((2 * rows, 2 * count * HEAD_SIZE), dtype)

    def sums(n):
        return [pltpu.VMEM((n * rows, HEAD_SIZE), f32)] * 2

    layout = (own_all, (prompt_mask, near))
    blocks = [*own_blocks, *prompt_blocks[:2]]
    stats = call(stats_kernel, layout, every, scalars, work, blocks, [], [stats_shape()], [], 2)[0]
    layout = ((prompt_mask, far),)
    outs = [stats_shape(), terms_shape(HEADS, bf16)]
    stats, terms_far = call(
        last_keys_kernel, layout, every, scalars, work, prompt_blocks[2:], [stats], outs, sums(2), 4
    )
    layout = ((prompt_mask, near),)
    outs = [terms_shape(HEADS, f32)]
    terms = call(
        terms_kernel, layout, every, scalars, work, prompt_blocks[:2], [stats], outs, sums(2), 4
    )[0]

    def plus(a, b):
        return a.astype(f32) + b.astype(f32)

    total = plus(terms, send(terms_far, 2)).astype(bf16)
    layout = (own_all, (prompt_mask, near + far))
    blocks = [*own_blocks, *prompt_blocks]
    att, dq, own_sums = [], [], []
    step, hop = 1, 0
    while step < seq_count:
        sends = [(i + step, i) for i in range(0, seq_count, 2 * step)]
        got = lax.ppermute(total, "seq", sends)
        if hop < HEADS:
            outs = [shape((rows, WIDTH), bf16)] * 4 + [terms_shape(1, f32), terms_shape(1, bf16)]
            a_m, a_s, d_m, d_s, own_near, own_far, token = call(
                rows_kernel, layout, (hop, one), scalars, work, blocks, [stats], outs, sums(4), 8, total
            )
            att.append((a_m, send(a_s, 1)))
            dq.append((d_m, send(d_s, 1)))
            own_sums.append((own_near, own_far))
            got = plus(got, token)
        total = plus(total, got).astype(bf16)
        step *= 2
        hop += 1

    def both_halves(parts):
        mine = jnp.concatenate([x for x, _ in parts], axis=1)
        theirs = jnp.concatenate([x for _, x in parts], axis=1)
        return jnp.where(
            core == 0,
            jnp.concatenate([mine, theirs], axis=1),
            jnp.concatenate([theirs, mine], axis=1),
        )

    attention, query_grad = both_halves(att), both_halves(dq)
    total = jnp.where(s == 0, total.astype(f32), jnp.float32(0.0))
    own_near, own_far = [jnp.concatenate(x, axis=1) for x in zip(*own_sums)]
    total = (plus(own_near, send(own_far, 2)) + total).astype(bf16)
    total = both_halves([(total[:rows], send(total[rows:], 1))])

    def gradient(first):
        parts = []
        for j in range(KEY_VALUE_HEADS):
            start = (2 * j + first) * HEAD_SIZE
            parts.append(total[:, start : start + HEAD_SIZE])
        return jnp.concatenate(parts, axis=1)

    return (attention, query_grad, gradient(0), gradient(1))


def solution(mesh):
    spec = P(("seq", "head"), None)
    return jax.shard_map(
        functools.partial(on_device, mesh.shape["seq"], mesh.shape["head"]),
        mesh=mesh,
        in_specs=(spec, spec, spec, spec, P("seq", None)),
        out_specs=(spec, spec, spec, spec),
        check_vma=False,
    )
```

```python
import functools
import math

import jax
import jax.numpy as jnp
from jax import lax
from jax.experimental import pallas as pl
from jax.experimental.pallas import tpu as pltpu
from jax.sharding import PartitionSpec as P

QUERY_HEADS = 28
KEY_VALUE_HEADS = 4
HEAD_SIZE = 128
GROUP = QUERY_HEADS // KEY_VALUE_HEADS
WIDTH = GROUP * HEAD_SIZE
HEADS = KEY_VALUE_HEADS // 2
SCALE = HEAD_SIZE ** (-0.5)
EXP2_SCALE = SCALE * math.log2(math.e)
MASKED = -1e30
VMEM_BYTES = 16 * 1024 * 1024


def dot_nt(a, b):
    return lax.dot_general(a, b, (((1,), (1,)), ((), ())), preferred_element_type=jnp.float32)


def dot_nn(a, b):
    return lax.dot_general(a, b, (((1,), (0,)), ((), ())), preferred_element_type=jnp.float32)


def group_rows(mine, sibling):
    parts = []
    for g in range(GROUP):
        columns = slice(g * HEAD_SIZE, (g + 1) * HEAD_SIZE)
        parts += [mine[:, columns], sibling[:, columns]]
    return jnp.concatenate(parts, axis=0)


def per_head(x):
    return jnp.concatenate([x] * GROUP, axis=1)


def own_bias(place, rows, ids, tree):
    h = ids[0]
    if place < 2:
        lane = lax.broadcasted_iota(jnp.int32, (rows, rows), 1)
        sub = lax.broadcasted_iota(jnp.int32, (rows, rows), 0)
        parts = []
        for a in range(2):
            ahead = lane - sub >= ((h ^ place) - (h ^ a)) * rows
            parts.append(jnp.where(ahead, jnp.float32(0.0), jnp.float32(MASKED)))
        return jnp.concatenate(parts, axis=1)
    return block_bias([(h ^ place) <= (h ^ a) for a in range(2)], rows)


def prompt_bias(place, rows, ids, tree):
    h, s = ids[0], ids[1]
    return block_bias([jnp.logical_and(tree[h ^ a, h ^ place] > 0, s > 0) for a in range(2)], rows)


def block_bias(reads, rows):
    lane = lax.broadcasted_iota(jnp.int32, (1, 2 * rows), 1)
    bias = [jnp.where(r, jnp.float32(0.0), jnp.float32(MASKED)) for r in reads]
    return jnp.where(lane < rows, bias[0], bias[1])


class Keys:
    def __init__(self, layout, ids, tree, qm, qs, cm, cs, refs):
        self.rows = qm.shape[0]
        self.q = group_rows(qm, qs)
        self.ct = group_rows(cm, cs)
        count = len(layout)
        self.keys = jnp.concatenate([b[:, :HEAD_SIZE] for b in refs[:count]], axis=0)
        self.values = jnp.concatenate([b[:, HEAD_SIZE:] for b in refs[:count]], axis=0)
        self.refs = refs[count:]
        self.bias = [bias(place, self.rows, ids, tree) for bias, place in layout]

    def blocks(self, x):
        return [x[i * self.rows : (i + 1) * self.rows] for i in range(len(self.bias))]

    def scores(self):
        out = []
        for x, bias in zip(self.blocks(dot_nt(self.keys, self.q)), self.bias):
            out.append(x if bias.shape[0] == 1 else x + per_head(bias))
        return out

    def dprobs(self):
        return self.blocks(dot_nt(self.values, self.ct))

    def top(self, scores):
        tops = []
        for x, bias in zip(scores, self.bias):
            top = jnp.max(x, axis=0, keepdims=True)
            tops.append(top + per_head(bias) if bias.shape[0] == 1 else top)
        return functools.reduce(jnp.maximum, tops)

    def weights(self, scores, top):
        out = []
        for x, bias in zip(scores, self.bias):
            row = top - per_head(bias) if bias.shape[0] == 1 else top
            out.append(jnp.exp2((x - row) * EXP2_SCALE))
        return out


def column_sum(parts):
    return functools.reduce(jnp.add, [jnp.sum(x, axis=0, keepdims=True) for x in parts])


def put_stats(stats, top, total, delta):
    stats[0, 0:1, :] = top
    stats[0, 1:2, :] = total
    stats[0, 2:3, :] = delta


def put_terms(out, dscore, probs, k):
    out[:, :HEAD_SIZE] = (dot_nn(dscore, k.q) * SCALE).astype(out.dtype)
    out[:, HEAD_SIZE:] = dot_nn(probs, k.ct).astype(out.dtype)


def rounded(parts):
    return jnp.concatenate([x.astype(jnp.bfloat16) for x in parts], axis=0)


def stats_kernel(layout, ids, tree, qm, qs, cm, cs, *refs):
    k = Keys(layout, ids, tree, qm, qs, cm, cs, refs)
    (stats,) = k.refs
    scores = k.scores()
    top = k.top(scores)
    e = k.weights(scores, top)
    delta = column_sum([x * y for x, y in zip(e, k.dprobs())])
    put_stats(stats, top, column_sum(e), delta)


def last_keys_kernel(layout, ids, tree, qm, qs, cm, cs, *refs):
    k = Keys(layout, ids, tree, qm, qs, cm, cs, refs)
    old, stats, terms = k.refs
    scores, dprobs = k.scores(), k.dprobs()
    old_top = old[0, 0:1, :]
    top = jnp.maximum(k.top(scores), old_top)
    keep = jnp.exp2((old_top - top) * EXP2_SCALE)
    e = k.weights(scores, top)
    inverse = 1.0 / (column_sum(e) + old[0, 1:2, :] * keep)
    delta = column_sum([x * y for x, y in zip(e, dprobs)]) + old[0, 2:3, :] * keep
    delta = delta * inverse
    put_stats(stats, top, inverse, delta)
    probs = [x * inverse for x in e]
    put_terms(terms, rounded([p * (d - delta) for p, d in zip(probs, dprobs)]), rounded(probs), k)


def probs_dscore(k, stats):
    inverse, delta = stats[0, 1:2, :], stats[0, 2:3, :]
    probs = [x * inverse for x in k.weights(k.scores(), stats[0, 0:1, :])]
    dscore = [p * (d - delta) for p, d in zip(probs, k.dprobs())]
    return rounded(probs), rounded(dscore)


def terms_kernel(layout, ids, tree, qm, qs, cm, cs, *refs):
    k = Keys(layout, ids, tree, qm, qs, cm, cs, refs)
    stats, terms = k.refs
    probs, dscore = probs_dscore(k, stats)
    put_terms(terms, dscore, probs, k)


def rows_kernel(layout, ids, tree, qm, qs, cm, cs, *refs):
    k = Keys(layout, ids, tree, qm, qs, cm, cs, refs)
    stats, _, att_m, att_s, dq_m, dq_s, near, far, token = k.refs
    token[...] = jnp.zeros_like(token)
    rows = k.rows
    probs, dscore = probs_dscore(k, stats)
    half = near.shape[0]
    put_terms(near, dscore[:half], probs[:half], k)
    put_terms(far, dscore[half : 2 * half], probs[half : 2 * half], k)
    att = dot_nn(k.values.T, probs)
    dq = dot_nn(k.keys.T, dscore) * SCALE
    for g in range(GROUP):
        columns = slice(g * HEAD_SIZE, (g + 1) * HEAD_SIZE)
        for i, (a, d) in enumerate(((att_m, dq_m), (att_s, dq_s))):
            part = slice((2 * g + i) * rows, (2 * g + i + 1) * rows)
            a[:, columns] = att[:, part].T.astype(jnp.bfloat16)
            d[:, columns] = dq[:, part].T.astype(jnp.bfloat16)


def call(kernel, layout, heads, scalars, work, blocks, inputs, outs, products, tie=None):
    rows = work[0].shape[0]
    first, count = heads

    def spec(shape, base):
        if len(shape) == 2:
            return pl.BlockSpec((shape[0], shape[1] // (HEADS if base is not None else count)), lambda i, *refs: (0, i + (base or 0)))
        return pl.BlockSpec((1, *shape[1:]), lambda i, *refs: (i + (base or 0),) + (0,) * (len(shape) - 1))

    sib = spec((rows, HEADS * WIDTH), first)
    specs = [sib] * 4 + [spec(x.shape, first) for x in (*blocks, *inputs)]
    operands = [*scalars, *work, *blocks, *inputs]
    out_specs = [spec(o.shape, None) for o in outs]
    if tie is not None:
        operands.append(tie)
        specs.append(pl.BlockSpec((16, HEAD_SIZE), lambda i, *refs: (0, 0)))
        outs = [*outs, jax.ShapeDtypeStruct(tie.shape, tie.dtype)]
        out_specs.append(pl.BlockSpec(tie.shape, lambda i, *refs: (0, 0)))
    flops = count * 2 * products * (2 * rows * GROUP) * (len(blocks) * rows) * HEAD_SIZE
    return pl.pallas_call(
        functools.partial(kernel, layout),
        grid_spec=pltpu.PrefetchScalarGridSpec(
            num_scalar_prefetch=2,
            grid=(count,),
            in_specs=specs,
            out_specs=out_specs,
        ),
        out_shape=outs,
        compiler_params=pltpu.CompilerParams(vmem_limit_bytes=VMEM_BYTES),
        cost_estimate=pl.CostEstimate(
            flops=flops, bytes_accessed=count * 4 * 2 * rows * WIDTH * 2, transcendentals=0
        ),
    )(*operands)


def after(x, *tokens):
    return lax.optimization_barrier((x, *tokens))[0]


def on_device(seq_count, head_count, queries, rotated_key_rows, value_matrix, cotangent, tree_mask):
    s = lax.axis_index("seq")
    h = lax.axis_index("head")
    rows = queries.shape[0]
    core = h & 1
    scalars = (jnp.stack([h, s]).astype(jnp.int32), tree_mask)
    f32, bf16 = jnp.float32, jnp.bfloat16
    shape = jax.ShapeDtypeStruct

    def send(x, mask):
        return lax.ppermute(x, "head", [(i, i ^ mask) for i in range(head_count)])

    def columns(x, place, width):
        return lax.dynamic_slice_in_dim(x, place * width, width, 1)

    def half(kv, place):
        k, v = [columns(x, place, HEADS * HEAD_SIZE) for x in kv]
        parts = []
        for j in range(HEADS):
            part = slice(j * HEAD_SIZE, (j + 1) * HEAD_SIZE)
            parts += [k[:, part], v[:, part]]
        return jnp.concatenate(parts, axis=1)

    def gathered(kv, place):
        mine, other = half(kv, place), half(kv, 1 - place)
        return [mine, send(other, 1), send(mine, 2), send(other, 3)]

    hops = [1]
    step = seq_count // 2
    while step > 1:
        hops.append(step)
        step //= 2
    held = (rotated_key_rows, value_matrix)
    for hop, step in enumerate(hops):
        reached = seq_count if hop == 0 else 2 * step
        sends = [(i, i + step) for i in range(0, seq_count, reached)]
        if hop:
            sends += [(i + 1, i + 1 + step) for i, _ in sends]
            place = s - s % 2
            got = lax.ppermute(held, "seq", sends)
        else:
            place = s
            got = jnp.concatenate([lax.ppermute(x, "seq", sends) for x in held], axis=1)
            held = lax.optimization_barrier(jnp.concatenate(held, axis=1))
        held = jnp.where(place % reached == step, got, held)
        if hop == 0:
            side = after(core, held[:16, :HEAD_SIZE])
            own_blocks = gathered((rotated_key_rows, value_matrix), side)
            q_sib = send(columns(queries, 1 - side, HEADS * WIDTH), 1)
            c_sib = send(columns(cotangent, 1 - side, HEADS * WIDTH), 1)
            q_mine, c_mine = [columns(x, side, HEADS * WIDTH) for x in (queries, cotangent)]
            work = (q_mine, q_sib, c_mine, c_sib)
    width = KEY_VALUE_HEADS * HEAD_SIZE
    prompt = (held[:, :width], held[:, width:])
    prompt_blocks = gathered(prompt, core)

    near, far = (0, 1), (2, 3)
    own_all = tuple((own_bias, b) for b in near + far)
    every, one = (0, HEADS), 1

    def stats_shape():
        return shape((HEADS, 8, 2 * GROUP * rows), f32)

    def terms_shape(count, dtype):
        return shape((2 * rows, 2 * count * HEAD_SIZE), dtype)

    layout = own_all + tuple((prompt_bias, b) for b in near)
    blocks = [*own_blocks, *prompt_blocks[:2]]
    stats = call(stats_kernel, layout, every, scalars, work, blocks, [], [stats_shape()], 2)[0]
    layout = tuple((prompt_bias, b) for b in far)
    outs = [stats_shape(), terms_shape(HEADS, bf16)]
    stats, terms_far = call(
        last_keys_kernel, layout, every, scalars, work, prompt_blocks[2:], [stats], outs, 4
    )
    layout = tuple((prompt_bias, b) for b in near)
    outs = [terms_shape(HEADS, bf16)]
    terms = call(
        terms_kernel, layout, every, scalars, work, prompt_blocks[:2], [stats], outs, 4
    )[0]

    def plus(a, b):
        return a.astype(f32) + b.astype(f32)

    def across(x, pairs):
        flat = []
        for h in range(head_count):
            flat += [(a * head_count + h, b * head_count + (h ^ mask)) for a, b, mask in pairs]
        return lax.ppermute(x, ("seq", "head"), flat)

    even = range(0, seq_count, 2)
    got_far = across(terms_far, [(i, i, 2) for i in even])
    got_next_far = across(terms_far, [(i + 1, i, 2) for i in even])
    got_next = across(terms, [(i + 1, i, 0) for i in even])
    layout = own_all + tuple((prompt_bias, b) for b in near + far)
    blocks = [*own_blocks, *prompt_blocks]
    att, dq, own_sums = [], [], []
    total, tie = None, terms
    step, hop = 1, 0
    while step < seq_count:
        if hop:
            got = lax.ppermute(total, "seq", [(i + step, i) for i in range(0, seq_count, 2 * step)])
        if hop < HEADS:
            outs = [shape((rows, WIDTH), bf16)] * 4 + [terms_shape(1, f32), terms_shape(1, bf16)]
            a_m, a_s, d_m, d_s, own_near, own_far, token = call(
                rows_kernel, layout, (hop, one), scalars, work, blocks, [stats], outs, 8, tie
            )
            att.append((a_m, send(a_s, 1)))
            dq.append((d_m, send(d_s, 1)))
            own_sums.append((own_near, own_far))
        else:
            token = jnp.zeros_like(total)
        if hop:
            total = total + (got + token)
        else:
            total = plus(plus(terms, got_far), plus(got_next_far, got_next)) + token.astype(f32)
            total = total.astype(bf16)
        tie = total
        step *= 2
        hop += 1

    def both_halves(parts):
        mine = jnp.concatenate([x for x, _ in parts], axis=1)
        theirs = jnp.concatenate([x for _, x in parts], axis=1)
        return jnp.where(
            core == 0,
            jnp.concatenate([mine, theirs], axis=1),
            jnp.concatenate([theirs, mine], axis=1),
        )

    attention, query_grad = both_halves(att), both_halves(dq)
    total = jnp.where(s == 0, total.astype(f32), jnp.float32(0.0))
    own_near, own_far = [jnp.concatenate(x, axis=1) for x in zip(*own_sums)]
    total = (plus(own_near, send(own_far, 2)) + total).astype(bf16)
    total = both_halves([(total[:rows], send(total[rows:], 1))])

    def gradient(first):
        parts = []
        for j in range(KEY_VALUE_HEADS):
            start = (2 * j + first) * HEAD_SIZE
            parts.append(total[:, start : start + HEAD_SIZE])
        return jnp.concatenate(parts, axis=1)

    return (attention, query_grad, gradient(0), gradient(1))


def solution(mesh):
    spec = P(("seq", "head"), None)
    return jax.shard_map(
        functools.partial(on_device, mesh.shape["seq"], mesh.shape["head"]),
        mesh=mesh,
        in_specs=(spec, spec, spec, spec, P("seq", None)),
        out_specs=(spec, spec, spec, spec),
        check_vma=False,
    )
```

```python
import functools
import math

import jax
import jax.numpy as jnp
from jax import lax
from jax.experimental import pallas as pl
from jax.experimental.pallas import tpu as pltpu
from jax.sharding import PartitionSpec as P

QUERY_HEADS = 28
KEY_VALUE_HEADS = 4
HEAD_SIZE = 128
GROUP = QUERY_HEADS // KEY_VALUE_HEADS
WIDTH = GROUP * HEAD_SIZE
HEADS = KEY_VALUE_HEADS // 2
SCALE = HEAD_SIZE ** (-0.5)
EXP2_SCALE = SCALE * math.log2(math.e)
MASKED = -1e30
VMEM_BYTES = 16 * 1024 * 1024


def dot_nt(a, b):
    return lax.dot_general(a, b, (((1,), (1,)), ((), ())), preferred_element_type=jnp.float32)


def dot_nn(a, b):
    return lax.dot_general(a, b, (((1,), (0,)), ((), ())), preferred_element_type=jnp.float32)


def group_rows(mine, sibling):
    parts = []
    for g in range(GROUP):
        columns = slice(g * HEAD_SIZE, (g + 1) * HEAD_SIZE)
        parts += [mine[:, columns], sibling[:, columns]]
    return jnp.concatenate(parts, axis=0)


def per_head(x):
    return jnp.concatenate([x] * GROUP, axis=1)


def own_bias(place, rows, ids, tree):
    h = ids[0]
    if place < 2:
        lane = lax.broadcasted_iota(jnp.int32, (rows, rows), 1)
        sub = lax.broadcasted_iota(jnp.int32, (rows, rows), 0)
        parts = []
        for a in range(2):
            ahead = lane - sub >= ((h ^ place) - (h ^ a)) * rows
            parts.append(jnp.where(ahead, jnp.float32(0.0), jnp.float32(MASKED)))
        return jnp.concatenate(parts, axis=1)
    return block_bias([(h ^ place) <= (h ^ a) for a in range(2)], rows)


def prompt_bias(place, rows, ids, tree):
    h, s = ids[0], ids[1]
    return block_bias([jnp.logical_and(tree[h ^ a, h ^ place] > 0, s > 0) for a in range(2)], rows)


def block_bias(reads, rows):
    lane = lax.broadcasted_iota(jnp.int32, (1, 2 * rows), 1)
    bias = [jnp.where(r, jnp.float32(0.0), jnp.float32(MASKED)) for r in reads]
    return jnp.where(lane < rows, bias[0], bias[1])


class Keys:
    def __init__(self, layout, ids, tree, qm, qs, cm, cs, refs):
        self.rows = qm.shape[0]
        self.q = group_rows(qm, qs)
        self.ct = group_rows(cm, cs)
        count = len(layout)
        self.keys = jnp.concatenate([b[:, :HEAD_SIZE] for b in refs[:count]], axis=0)
        self.values = jnp.concatenate([b[:, HEAD_SIZE:] for b in refs[:count]], axis=0)
        self.refs = refs[count:]
        self.bias = [bias(place, self.rows, ids, tree) for bias, place in layout]

    def blocks(self, x):
        return [x[i * self.rows : (i + 1) * self.rows] for i in range(len(self.bias))]

    def scores(self):
        out = []
        for x, bias in zip(self.blocks(dot_nt(self.keys, self.q)), self.bias):
            out.append(x if bias.shape[0] == 1 else x + per_head(bias))
        return out

    def dprobs(self):
        return self.blocks(dot_nt(self.values, self.ct))

    def top(self, scores):
        tops = []
        for x, bias in zip(scores, self.bias):
            top = jnp.max(x, axis=0, keepdims=True)
            tops.append(top + per_head(bias) if bias.shape[0] == 1 else top)
        return functools.reduce(jnp.maximum, tops)

    def weights(self, scores, top):
        out = []
        for x, bias in zip(scores, self.bias):
            row = top - per_head(bias) if bias.shape[0] == 1 else top
            out.append(jnp.exp2((x - row) * EXP2_SCALE))
        return out


def column_sum(parts):
    return functools.reduce(jnp.add, [jnp.sum(x, axis=0, keepdims=True) for x in parts])


def put_stats(stats, top, total, delta):
    stats[0, 0:1, :] = top
    stats[0, 1:2, :] = total
    stats[0, 2:3, :] = delta


def put_terms(out, dscore, probs, k):
    out[:, :HEAD_SIZE] = (dot_nn(dscore, k.q) * SCALE).astype(out.dtype)
    out[:, HEAD_SIZE:] = dot_nn(probs, k.ct).astype(out.dtype)


def rounded(parts):
    return jnp.concatenate([x.astype(jnp.bfloat16) for x in parts], axis=0)


def stats_kernel(layout, ids, tree, qm, qs, cm, cs, *refs):
    k = Keys(layout, ids, tree, qm, qs, cm, cs, refs)
    (stats,) = k.refs
    scores = k.scores()
    top = k.top(scores)
    e = k.weights(scores, top)
    delta = column_sum([x * y for x, y in zip(e, k.dprobs())])
    put_stats(stats, top, column_sum(e), delta)


def last_keys_kernel(layout, ids, tree, qm, qs, cm, cs, *refs):
    k = Keys(layout, ids, tree, qm, qs, cm, cs, refs)
    old, stats, terms = k.refs
    scores, dprobs = k.scores(), k.dprobs()
    old_top = old[0, 0:1, :]
    top = jnp.maximum(k.top(scores), old_top)
    keep = jnp.exp2((old_top - top) * EXP2_SCALE)
    e = k.weights(scores, top)
    inverse = 1.0 / (column_sum(e) + old[0, 1:2, :] * keep)
    delta = column_sum([x * y for x, y in zip(e, dprobs)]) + old[0, 2:3, :] * keep
    delta = delta * inverse
    put_stats(stats, top, inverse, delta)
    probs = [x * inverse for x in e]
    put_terms(terms, rounded([p * (d - delta) for p, d in zip(probs, dprobs)]), rounded(probs), k)


def probs_dscore(k, stats):
    inverse, delta = stats[0, 1:2, :], stats[0, 2:3, :]
    probs = [x * inverse for x in k.weights(k.scores(), stats[0, 0:1, :])]
    dscore = [p * (d - delta) for p, d in zip(probs, k.dprobs())]
    return rounded(probs), rounded(dscore)


def terms_kernel(layout, ids, tree, qm, qs, cm, cs, *refs):
    k = Keys(layout, ids, tree, qm, qs, cm, cs, refs)
    stats, terms = k.refs
    probs, dscore = probs_dscore(k, stats)
    put_terms(terms, dscore, probs, k)


def rows_kernel(layout, ids, tree, qm, qs, cm, cs, *refs):
    k = Keys(layout, ids, tree, qm, qs, cm, cs, refs)
    stats, _, att_m, att_s, dq_m, dq_s, near, far, token = k.refs
    token[...] = jnp.zeros_like(token)
    rows = k.rows
    probs, dscore = probs_dscore(k, stats)
    half = near.shape[0]
    put_terms(near, dscore[:half], probs[:half], k)
    put_terms(far, dscore[half : 2 * half], probs[half : 2 * half], k)
    att = dot_nn(k.values.T, probs)
    dq = dot_nn(k.keys.T, dscore) * SCALE
    for g in range(GROUP):
        columns = slice(g * HEAD_SIZE, (g + 1) * HEAD_SIZE)
        for i, (a, d) in enumerate(((att_m, dq_m), (att_s, dq_s))):
            part = slice((2 * g + i) * rows, (2 * g + i + 1) * rows)
            a[:, columns] = att[:, part].T.astype(jnp.bfloat16)
            d[:, columns] = dq[:, part].T.astype(jnp.bfloat16)


def halves_kernel(side, q, c, q_mine, q_other, c_mine, c_other, done):
    width = q_mine.shape[1]
    copies = []
    for x, out, place in (
        (q, q_other, 1 - side[0]),
        (c, c_other, 1 - side[0]),
        (q, q_mine, side[0]),
        (c, c_mine, side[0]),
    ):
        part = pl.ds(pl.multiple_of(place * width, HEAD_SIZE), width)
        copies.append(pltpu.make_async_copy(x.at[:, part], out, done.at[len(copies)]))
    for copy in copies:
        copy.start()
    for copy in copies:
        copy.wait()


def halves(side, q, c):
    half = jax.ShapeDtypeStruct((q.shape[0], q.shape[1] // 2), q.dtype)
    hbm = pl.BlockSpec(memory_space=pltpu.MemorySpace.HBM)
    return pl.pallas_call(
        halves_kernel,
        in_specs=[pl.BlockSpec(memory_space=pltpu.SMEM), hbm, hbm],
        out_specs=[pl.BlockSpec(memory_space=pltpu.VMEM)] * 4,
        out_shape=[half] * 4,
        scratch_shapes=[pltpu.SemaphoreType.DMA((4,))],
        cost_estimate=pl.CostEstimate(flops=0, bytes_accessed=8 * q.size, transcendentals=0),
    )(side.astype(jnp.int32).reshape(1), q, c)


def call(kernel, layout, heads, scalars, work, blocks, inputs, outs, products, tie=None):
    rows = work[0].shape[0]
    first, count = heads
    ins = [*work, *blocks, *inputs]
    if tie is not None:
        ins.append(tie)
        outs = [*outs, jax.ShapeDtypeStruct(tie.shape, tie.dtype)]

    def part(ref, j, held):
        if len(ref.shape) == 3:
            return ref.at[j : j + 1]
        width = ref.shape[1] // held
        return ref.at[:, j * width : (j + 1) * width]

    def body(ids, tree, *refs):
        given, made = refs[: len(ins)], refs[len(ins) :]
        for i in range(count):
            views = [part(r, first + i, HEADS) for r in given] + [part(r, i, count) for r in made]
            if tie is not None:
                views[len(ins) - 1], views[-1] = given[-1], made[-1]
            kernel(layout, ids, tree, *views)

    vmem = pl.BlockSpec(memory_space=pltpu.VMEM)
    smem = pl.BlockSpec(memory_space=pltpu.SMEM)
    specs = [smem, smem, *[vmem] * len(ins)]
    if tie is not None:
        specs[-1] = pl.BlockSpec(memory_space=pl.ANY)
    flops = count * 2 * products * (2 * rows * GROUP) * (len(blocks) * rows) * HEAD_SIZE
    return pl.pallas_call(
        body,
        in_specs=specs,
        out_specs=[vmem] * len(outs),
        out_shape=outs,
        compiler_params=pltpu.CompilerParams(vmem_limit_bytes=VMEM_BYTES),
        cost_estimate=pl.CostEstimate(
            flops=flops, bytes_accessed=count * 4 * 2 * rows * WIDTH * 2, transcendentals=0
        ),
    )(*scalars, *ins)


def after(x, *tokens):
    return lax.optimization_barrier((x, *tokens))[0]


def on_device(seq_count, head_count, queries, rotated_key_rows, value_matrix, cotangent, tree_mask):
    s = lax.axis_index("seq")
    h = lax.axis_index("head")
    rows = queries.shape[0]
    core = h & 1
    scalars = (jnp.stack([h, s]).astype(jnp.int32), tree_mask)
    f32, bf16 = jnp.float32, jnp.bfloat16
    shape = jax.ShapeDtypeStruct

    def send(x, mask):
        return lax.ppermute(x, "head", [(i, i ^ mask) for i in range(head_count)])

    def columns(x, place, width):
        return lax.dynamic_slice_in_dim(x, place * width, width, 1)

    def half(kv, place):
        k, v = [columns(x, place, HEADS * HEAD_SIZE) for x in kv]
        parts = []
        for j in range(HEADS):
            part = slice(j * HEAD_SIZE, (j + 1) * HEAD_SIZE)
            parts += [k[:, part], v[:, part]]
        return jnp.concatenate(parts, axis=1)

    def gathered(kv, place):
        mine, other = half(kv, place), half(kv, 1 - place)
        return [mine, send(other, 1), send(mine, 2), send(other, 3)]

    hops = [1]
    step = seq_count // 2
    while step > 1:
        hops.append(step)
        step //= 2
    held = (rotated_key_rows, value_matrix)
    for hop, step in enumerate(hops):
        reached = seq_count if hop == 0 else 2 * step
        sends = [(i, i + step) for i in range(0, seq_count, reached)]
        if hop:
            sends += [(i + 1, i + 1 + step) for i, _ in sends]
            place = s - s % 2
            got = lax.ppermute(held, "seq", sends)
        else:
            place = s
            got = jnp.concatenate([lax.ppermute(x, "seq", sends) for x in held], axis=1)
            held = lax.optimization_barrier(jnp.concatenate(held, axis=1))
        held = jnp.where(place % reached == step, got, held)
        if hop == 0:
            side = after(core, held[:16, :HEAD_SIZE])
            own_blocks = gathered((rotated_key_rows, value_matrix), side)
            q_mine, q_other, c_mine, c_other = halves(side, queries, cotangent)
            q_sib, c_sib = send(q_other, 1), send(c_other, 1)
        if hop == 1:
            held, q_mine, q_sib, c_sib = lax.optimization_barrier((held, q_mine, q_sib, c_sib))
    width = KEY_VALUE_HEADS * HEAD_SIZE
    prompt = (held[:, :width], held[:, width:])
    work = (q_mine, q_sib, c_mine, c_sib)
    prompt_blocks = gathered(prompt, core)

    near, far = (0, 1), (2, 3)
    own_all = tuple((own_bias, b) for b in near + far)
    every, one = (0, HEADS), 1

    def stats_shape():
        return shape((HEADS, 8, 2 * GROUP * rows), f32)

    def terms_shape(count, dtype):
        return shape((2 * rows, 2 * count * HEAD_SIZE), dtype)

    layout = own_all + tuple((prompt_bias, b) for b in near)
    blocks = [*own_blocks, *prompt_blocks[:2]]
    stats = call(stats_kernel, layout, every, scalars, work, blocks, [], [stats_shape()], 2)[0]
    layout = tuple((prompt_bias, b) for b in far)
    outs = [stats_shape(), terms_shape(HEADS, bf16)]
    stats, terms_far = call(
        last_keys_kernel, layout, every, scalars, work, prompt_blocks[2:], [stats], outs, 4
    )
    layout = tuple((prompt_bias, b) for b in near)
    outs = [terms_shape(HEADS, bf16)]
    terms = call(
        terms_kernel, layout, every, scalars, work, prompt_blocks[:2], [stats], outs, 4
    )[0]

    def plus(a, b):
        return a.astype(f32) + b.astype(f32)

    def across(x, pairs):
        flat = []
        for h in range(head_count):
            flat += [(a * head_count + h, b * head_count + (h ^ mask)) for a, b, mask in pairs]
        return lax.ppermute(x, ("seq", "head"), flat)

    even = range(0, seq_count, 2)
    got_far = across(terms_far, [(i, i, 2) for i in even])
    got_next_far = across(terms_far, [(i + 1, i, 2) for i in even])
    got_next = across(terms, [(i + 1, i, 0) for i in even])
    layout = own_all + tuple((prompt_bias, b) for b in near + far)
    blocks = [*own_blocks, *prompt_blocks]
    att, dq, own_sums = [], [], []
    total, tie = None, terms
    step, hop = 1, 0
    while step < seq_count:
        if hop:
            got = lax.ppermute(total, "seq", [(i + step, i) for i in range(0, seq_count, 2 * step)])
        if hop < HEADS:
            outs = [shape((rows, WIDTH), bf16)] * 4 + [terms_shape(1, f32), terms_shape(1, bf16)]
            a_m, a_s, d_m, d_s, own_near, own_far, token = call(
                rows_kernel, layout, (hop, one), scalars, work, blocks, [stats], outs, 8, tie
            )
            att.append((a_m, send(a_s, 1)))
            dq.append((d_m, send(d_s, 1)))
            own_sums.append((own_near, own_far))
        else:
            token = jnp.zeros_like(total)
        if hop:
            total = total + (got + token)
        else:
            total = plus(plus(terms, got_far), plus(got_next_far, got_next)) + token.astype(f32)
            total = total.astype(bf16)
        tie = total
        step *= 2
        hop += 1

    def both_halves(parts):
        mine = jnp.concatenate([x for x, _ in parts], axis=1)
        theirs = jnp.concatenate([x for _, x in parts], axis=1)
        return jnp.where(
            core == 0,
            jnp.concatenate([mine, theirs], axis=1),
            jnp.concatenate([theirs, mine], axis=1),
        )

    attention, query_grad = both_halves(att), both_halves(dq)
    total = jnp.where(s == 0, total.astype(f32), jnp.float32(0.0))
    own_near, own_far = [jnp.concatenate(x, axis=1) for x in zip(*own_sums)]
    total = (plus(own_near, send(own_far, 2)) + total).astype(bf16)
    total = both_halves([(total[:rows], send(total[rows:], 1))])

    def gradient(first):
        parts = []
        for j in range(KEY_VALUE_HEADS):
            start = (2 * j + first) * HEAD_SIZE
            parts.append(total[:, start : start + HEAD_SIZE])
        return jnp.concatenate(parts, axis=1)

    return (attention, query_grad, gradient(0), gradient(1))


def solution(mesh):
    spec = P(("seq", "head"), None)
    return jax.shard_map(
        functools.partial(on_device, mesh.shape["seq"], mesh.shape["head"]),
        mesh=mesh,
        in_specs=(spec, spec, spec, spec, P("seq", None)),
        out_specs=(spec, spec, spec, spec),
        check_vma=False,
    )
```

```python
import functools
import math

import jax
import jax.numpy as jnp
from jax import lax
from jax.experimental import pallas as pl
from jax.experimental.pallas import tpu as pltpu
from jax.sharding import PartitionSpec as P

QUERY_HEADS = 28
KEY_VALUE_HEADS = 4
HEAD_SIZE = 128
GROUP = QUERY_HEADS // KEY_VALUE_HEADS
WIDTH = GROUP * HEAD_SIZE
HEADS = KEY_VALUE_HEADS // 2
SCALE = HEAD_SIZE ** (-0.5)
EXP2_SCALE = SCALE * math.log2(math.e)
MASKED = -1e30
VMEM_BYTES = 32 * 1024 * 1024


def dot_nt(a, b):
    return lax.dot_general(a, b, (((1,), (1,)), ((), ())), preferred_element_type=jnp.float32)


def dot_nn(a, b):
    return lax.dot_general(a, b, (((1,), (0,)), ((), ())), preferred_element_type=jnp.float32)


def group_rows(mine, sibling):
    parts = []
    for g in range(GROUP):
        columns = slice(g * HEAD_SIZE, (g + 1) * HEAD_SIZE)
        parts += [mine[:, columns], sibling[:, columns]]
    return jnp.concatenate(parts, axis=0)


def per_head(x):
    return jnp.concatenate([x] * GROUP, axis=1)


def own_bias(place, rows, ids, tree):
    h = ids[0]
    if place < 2:
        lane = lax.broadcasted_iota(jnp.int32, (rows, rows), 1)
        sub = lax.broadcasted_iota(jnp.int32, (rows, rows), 0)
        parts = []
        for a in range(2):
            ahead = lane - sub >= ((h ^ place) - (h ^ a)) * rows
            parts.append(jnp.where(ahead, jnp.float32(0.0), jnp.float32(MASKED)))
        return jnp.concatenate(parts, axis=1)
    return block_bias([(h ^ place) <= (h ^ a) for a in range(2)], rows)


def prompt_bias(place, rows, ids, tree):
    h, s = ids[0], ids[1]
    return block_bias([jnp.logical_and(tree[h ^ a, h ^ place] > 0, s > 0) for a in range(2)], rows)


def block_bias(reads, rows):
    lane = lax.broadcasted_iota(jnp.int32, (1, 2 * rows), 1)
    bias = [jnp.where(r, jnp.float32(0.0), jnp.float32(MASKED)) for r in reads]
    return jnp.where(lane < rows, bias[0], bias[1])


class Keys:
    def __init__(self, layout, ids, tree, qm, qs, cm, cs, refs):
        self.rows = qm.shape[0]
        self.q = group_rows(qm, qs)
        self.ct = group_rows(cm, cs)
        count = len(layout)
        self.keys = jnp.concatenate([b[:, :HEAD_SIZE] for b in refs[:count]], axis=0)
        self.values = jnp.concatenate([b[:, HEAD_SIZE:] for b in refs[:count]], axis=0)
        self.refs = refs[count:]
        self.bias = [bias(place, self.rows, ids, tree) for bias, place in layout]

    def blocks(self, x):
        return [x[i * self.rows : (i + 1) * self.rows] for i in range(len(self.bias))]

    def scores(self):
        out = []
        for x, bias in zip(self.blocks(dot_nt(self.keys, self.q)), self.bias):
            out.append(x if bias.shape[0] == 1 else x + per_head(bias))
        return out

    def dprobs(self):
        return self.blocks(dot_nt(self.values, self.ct))

    def top(self, scores):
        tops = []
        for x, bias in zip(scores, self.bias):
            top = jnp.max(x, axis=0, keepdims=True)
            tops.append(top + per_head(bias) if bias.shape[0] == 1 else top)
        return functools.reduce(jnp.maximum, tops)

    def weights(self, scores, top):
        out = []
        for x, bias in zip(scores, self.bias):
            row = top - per_head(bias) if bias.shape[0] == 1 else top
            out.append(jnp.exp2((x - row) * EXP2_SCALE))
        return out


def column_sum(parts):
    return functools.reduce(jnp.add, [jnp.sum(x, axis=0, keepdims=True) for x in parts])


def put_stats(stats, top, total, delta):
    stats[0, 0:1, :] = top
    stats[0, 1:2, :] = total
    stats[0, 2:3, :] = delta


def put_terms(out, dscore, probs, k):
    out[:, :HEAD_SIZE] = (dot_nn(dscore, k.q) * SCALE).astype(out.dtype)
    out[:, HEAD_SIZE:] = dot_nn(probs, k.ct).astype(out.dtype)


def rounded(parts):
    return jnp.concatenate([x.astype(jnp.bfloat16) for x in parts], axis=0)


def put_rows(x, mine, sibling, rows):
    for g in range(GROUP):
        columns = slice(g * HEAD_SIZE, (g + 1) * HEAD_SIZE)
        for i, out in enumerate((mine, sibling)):
            part = slice((2 * g + i) * rows, (2 * g + i + 1) * rows)
            out[:, columns] = x[:, part].T.astype(out.dtype)


def forward_kernel(layout, ids, tree, qm, qs, cm, cs, *refs):
    k = Keys(layout, ids, tree, qm, qs, cm, cs, refs)
    stats, terms, att_m, att_s = k.refs
    scores = k.scores()
    top = k.top(scores)
    e = k.weights(scores, top)
    inverse = 1.0 / column_sum(e)
    probs = [x * inverse for x in e]
    all_rounded = rounded(probs)
    att = dot_nn(k.values.T, all_rounded).astype(jnp.bfloat16).astype(jnp.float32)
    delta = jnp.sum(att * k.ct.T.astype(jnp.float32), axis=0, keepdims=True)
    put_stats(stats, top, inverse, delta)
    last = terms.shape[0] // k.rows
    dprobs = dot_nt(k.values[-terms.shape[0] :], k.ct)
    dprobs = [dprobs[i * k.rows : (i + 1) * k.rows] for i in range(last)]
    dscore = rounded([p * (d - delta) for p, d in zip(probs[-last:], dprobs)])
    put_terms(terms, dscore, all_rounded[-terms.shape[0] :], k)
    put_rows(att, att_m, att_s, k.rows)


def probs_dscore(k, stats):
    inverse, delta = stats[0, 1:2, :], stats[0, 2:3, :]
    probs = [x * inverse for x in k.weights(k.scores(), stats[0, 0:1, :])]
    dscore = [p * (d - delta) for p, d in zip(probs, k.dprobs())]
    return rounded(probs), rounded(dscore)


def terms_kernel(layout, ids, tree, qm, qs, cm, cs, *refs):
    k = Keys(layout, ids, tree, qm, qs, cm, cs, refs)
    stats, terms = k.refs
    probs, dscore = probs_dscore(k, stats)
    put_terms(terms, dscore, probs, k)


def rows_kernel(layout, ids, tree, qm, qs, cm, cs, *refs):
    k = Keys(layout, ids, tree, qm, qs, cm, cs, refs)
    stats, _, dq_m, dq_s, near, far, token = k.refs
    token[...] = jnp.zeros_like(token)
    rows = k.rows
    probs, dscore = probs_dscore(k, stats)
    half = near.shape[0]
    put_terms(near, dscore[:half], probs[:half], k)
    put_terms(far, dscore[half : 2 * half], probs[half : 2 * half], k)
    put_rows(dot_nn(k.keys.T, dscore) * SCALE, dq_m, dq_s, rows)


def halves_kernel(side, q, c, q_mine, q_other, c_mine, c_other, done):
    width = q_mine.shape[1]
    copies = []
    for x, out, place in (
        (q, q_other, 1 - side[0]),
        (c, c_other, 1 - side[0]),
        (q, q_mine, side[0]),
        (c, c_mine, side[0]),
    ):
        part = pl.ds(pl.multiple_of(place * width, HEAD_SIZE), width)
        copies.append(pltpu.make_async_copy(x.at[:, part], out, done.at[len(copies)]))
    for copy in copies:
        copy.start()
    for copy in copies:
        copy.wait()


def halves(side, q, c):
    half = jax.ShapeDtypeStruct((q.shape[0], q.shape[1] // 2), q.dtype)
    hbm = pl.BlockSpec(memory_space=pltpu.MemorySpace.HBM)
    return pl.pallas_call(
        halves_kernel,
        in_specs=[pl.BlockSpec(memory_space=pltpu.SMEM), hbm, hbm],
        out_specs=[pl.BlockSpec(memory_space=pltpu.VMEM)] * 4,
        out_shape=[half] * 4,
        scratch_shapes=[pltpu.SemaphoreType.DMA((4,))],
        cost_estimate=pl.CostEstimate(flops=0, bytes_accessed=8 * q.size, transcendentals=0),
    )(side.astype(jnp.int32).reshape(1), q, c)


def call(kernel, layout, heads, scalars, work, blocks, inputs, outs, products, tie=None):
    rows = work[0].shape[0]
    first, count = heads
    ins = [*work, *blocks, *inputs]
    if tie is not None:
        ins.append(tie)
        outs = [*outs, jax.ShapeDtypeStruct(tie.shape, tie.dtype)]

    def part(ref, j, held):
        if len(ref.shape) == 3:
            return ref.at[j : j + 1]
        width = ref.shape[1] // held
        return ref.at[:, j * width : (j + 1) * width]

    def body(ids, tree, *refs):
        given, made = refs[: len(ins)], refs[len(ins) :]
        for i in range(count):
            views = [part(r, first + i, HEADS) for r in given] + [part(r, i, count) for r in made]
            if tie is not None:
                views[len(ins) - 1], views[-1] = given[-1], made[-1]
            kernel(layout, ids, tree, *views)

    vmem = pl.BlockSpec(memory_space=pltpu.VMEM)
    smem = pl.BlockSpec(memory_space=pltpu.SMEM)
    specs = [smem, smem, *[vmem] * len(ins)]
    if tie is not None:
        specs[-1] = pl.BlockSpec(memory_space=pl.ANY)
    flops = count * 2 * products * (2 * rows * GROUP) * (len(blocks) * rows) * HEAD_SIZE
    return pl.pallas_call(
        body,
        in_specs=specs,
        out_specs=[vmem] * len(outs),
        out_shape=outs,
        compiler_params=pltpu.CompilerParams(vmem_limit_bytes=VMEM_BYTES),
        cost_estimate=pl.CostEstimate(
            flops=flops, bytes_accessed=count * 4 * 2 * rows * WIDTH * 2, transcendentals=0
        ),
    )(*scalars, *ins)


def after(x, *tokens):
    return lax.optimization_barrier((x, *tokens))[0]


def on_device(seq_count, head_count, queries, rotated_key_rows, value_matrix, cotangent, tree_mask):
    s = lax.axis_index("seq")
    h = lax.axis_index("head")
    rows = queries.shape[0]
    core = h & 1
    scalars = (jnp.stack([h, s]).astype(jnp.int32), tree_mask)
    f32, bf16 = jnp.float32, jnp.bfloat16
    shape = jax.ShapeDtypeStruct

    def send(x, mask):
        return lax.ppermute(x, "head", [(i, i ^ mask) for i in range(head_count)])

    def columns(x, place, width):
        return lax.dynamic_slice_in_dim(x, place * width, width, 1)

    def half(kv, place):
        k, v = [columns(x, place, HEADS * HEAD_SIZE) for x in kv]
        parts = []
        for j in range(HEADS):
            part = slice(j * HEAD_SIZE, (j + 1) * HEAD_SIZE)
            parts += [k[:, part], v[:, part]]
        return jnp.concatenate(parts, axis=1)

    def gathered(kv, place):
        mine, other = half(kv, place), half(kv, 1 - place)
        return [mine, send(other, 1), send(mine, 2), send(other, 3)]

    hops = [1]
    step = seq_count // 2
    while step > 1:
        hops.append(step)
        step //= 2
    held = (rotated_key_rows, value_matrix)
    for hop, step in enumerate(hops):
        reached = seq_count if hop == 0 else 2 * step
        sends = [(i, i + step) for i in range(0, seq_count, reached)]
        if hop:
            sends += [(i + 1, i + 1 + step) for i, _ in sends]
            place = s - s % 2
            got = lax.ppermute(held, "seq", sends)
        else:
            place = s
            got = jnp.concatenate([lax.ppermute(x, "seq", sends) for x in held], axis=1)
            held = lax.optimization_barrier(jnp.concatenate(held, axis=1))
        held = jnp.where(place % reached == step, got, held)
        if hop == 0:
            side = after(core, held[:16, :HEAD_SIZE])
            own_blocks = gathered((rotated_key_rows, value_matrix), side)
            q_mine, q_other, c_mine, c_other = halves(side, queries, cotangent)
            q_sib, c_sib = send(q_other, 1), send(c_other, 1)
        if hop == 1:
            held, q_mine, q_sib, c_sib = lax.optimization_barrier((held, q_mine, q_sib, c_sib))
    width = KEY_VALUE_HEADS * HEAD_SIZE
    prompt = (held[:, :width], held[:, width:])
    work = (q_mine, q_sib, c_mine, c_sib)
    prompt_blocks = gathered(prompt, core)

    near, far = (0, 1), (2, 3)
    own_all = tuple((own_bias, b) for b in near + far)
    every, one = (0, HEADS), 1

    def stats_shape():
        return shape((HEADS, 8, 2 * GROUP * rows), f32)

    def terms_shape(count, dtype):
        return shape((2 * rows, 2 * count * HEAD_SIZE), dtype)

    layout = own_all + tuple((prompt_bias, b) for b in near + far)
    blocks = [*own_blocks, *prompt_blocks]
    rows_shape = shape((rows, HEADS * WIDTH), bf16)
    outs = [stats_shape(), terms_shape(HEADS, bf16), rows_shape, rows_shape]
    stats, terms_far, att_m, att_s = call(
        forward_kernel, layout, every, scalars, work, blocks, [], outs, 5
    )
    layout = tuple((prompt_bias, b) for b in near)
    outs = [terms_shape(HEADS, bf16)]
    terms = call(
        terms_kernel, layout, every, scalars, work, prompt_blocks[:2], [stats], outs, 4
    )[0]

    def plus(a, b):
        return a.astype(f32) + b.astype(f32)

    def across(x, pairs):
        flat = []
        for h in range(head_count):
            flat += [(a * head_count + h, b * head_count + (h ^ mask)) for a, b, mask in pairs]
        return lax.ppermute(x, ("seq", "head"), flat)

    even = range(0, seq_count, 2)
    got_far = across(terms_far, [(i, i, 2) for i in even])
    got_next_far = across(terms_far, [(i + 1, i, 2) for i in even])
    got_next = across(terms, [(i + 1, i, 0) for i in even])
    layout = own_all + tuple((prompt_bias, b) for b in near + far)
    blocks = [*own_blocks, *prompt_blocks]
    dq, own_sums = [], []
    total, tie = None, terms
    step, hop = 1, 0
    while step < seq_count:
        if hop:
            got = lax.ppermute(total, "seq", [(i + step, i) for i in range(0, seq_count, 2 * step)])
        if hop < HEADS:
            outs = [shape((rows, WIDTH), bf16)] * 2 + [terms_shape(1, f32), terms_shape(1, bf16)]
            d_m, d_s, own_near, own_far, token = call(
                rows_kernel, layout, (hop, one), scalars, work, blocks, [stats], outs, 8, tie
            )
            dq.append((d_m, send(d_s, 1)))
            own_sums.append((own_near, own_far))
        else:
            token = jnp.zeros_like(total)
        if hop:
            total = total + (got + token)
        else:
            total = plus(plus(terms, got_far), plus(got_next_far, got_next)) + token.astype(f32)
            total = total.astype(bf16)
        tie = total
        step *= 2
        hop += 1

    def both_halves(parts):
        mine = jnp.concatenate([x for x, _ in parts], axis=1)
        theirs = jnp.concatenate([x for _, x in parts], axis=1)
        return jnp.where(
            core == 0,
            jnp.concatenate([mine, theirs], axis=1),
            jnp.concatenate([theirs, mine], axis=1),
        )

    attention, query_grad = both_halves([(att_m, send(att_s, 1))]), both_halves(dq)
    total = jnp.where(s == 0, total.astype(f32), jnp.float32(0.0))
    own_near, own_far = [jnp.concatenate(x, axis=1) for x in zip(*own_sums)]
    total = (plus(own_near, send(own_far, 2)) + total).astype(bf16)
    total = both_halves([(total[:rows], send(total[rows:], 1))])

    def gradient(first):
        parts = []
        for j in range(KEY_VALUE_HEADS):
            start = (2 * j + first) * HEAD_SIZE
            parts.append(total[:, start : start + HEAD_SIZE])
        return jnp.concatenate(parts, axis=1)

    return (attention, query_grad, gradient(0), gradient(1))


def solution(mesh):
    spec = P(("seq", "head"), None)
    return jax.shard_map(
        functools.partial(on_device, mesh.shape["seq"], mesh.shape["head"]),
        mesh=mesh,
        in_specs=(spec, spec, spec, spec, P("seq", None)),
        out_specs=(spec, spec, spec, spec),
        check_vma=False,
    )
```

```python
import functools
import math

import jax
import jax.numpy as jnp
from jax import lax
from jax.experimental import pallas as pl
from jax.experimental.pallas import tpu as pltpu
from jax.sharding import PartitionSpec as P

QUERY_HEADS = 28
KEY_VALUE_HEADS = 4
HEAD_SIZE = 128
GROUP = QUERY_HEADS // KEY_VALUE_HEADS
WIDTH = GROUP * HEAD_SIZE
HEADS = KEY_VALUE_HEADS // 2
SCALE = HEAD_SIZE ** (-0.5)
EXP2_SCALE = SCALE * math.log2(math.e)
MASKED = -1e30
VMEM_BYTES = 32 * 1024 * 1024


def dot_nt(a, b):
    return lax.dot_general(a, b, (((1,), (1,)), ((), ())), preferred_element_type=jnp.float32)


def dot_nn(a, b):
    return lax.dot_general(a, b, (((1,), (0,)), ((), ())), preferred_element_type=jnp.float32)


def group_rows(mine, sibling):
    parts = []
    for g in range(GROUP):
        columns = slice(g * HEAD_SIZE, (g + 1) * HEAD_SIZE)
        parts += [mine[:, columns], sibling[:, columns]]
    return jnp.concatenate(parts, axis=0)


def per_head(x):
    return jnp.concatenate([x] * GROUP, axis=1)


def own_bias(place, rows, ids, tree):
    h = ids[0]
    if place < 2:
        lane = lax.broadcasted_iota(jnp.int32, (rows, rows), 1)
        sub = lax.broadcasted_iota(jnp.int32, (rows, rows), 0)
        parts = []
        for a in range(2):
            ahead = lane - sub >= ((h ^ place) - (h ^ a)) * rows
            parts.append(jnp.where(ahead, jnp.float32(0.0), jnp.float32(MASKED)))
        return jnp.concatenate(parts, axis=1)
    return block_bias([(h ^ place) <= (h ^ a) for a in range(2)], rows)


def prompt_bias(place, rows, ids, tree):
    h, s = ids[0], ids[1]
    return block_bias([jnp.logical_and(tree[h ^ a, h ^ place] > 0, s > 0) for a in range(2)], rows)


def block_bias(reads, rows):
    lane = lax.broadcasted_iota(jnp.int32, (1, 2 * rows), 1)
    bias = [jnp.where(r, jnp.float32(0.0), jnp.float32(MASKED)) for r in reads]
    return jnp.where(lane < rows, bias[0], bias[1])


class Keys:
    def __init__(self, layout, ids, tree, qm, qs, cm, cs, refs):
        self.rows = qm.shape[0]
        self.q = group_rows(qm, qs)
        self.ct = group_rows(cm, cs)
        count = len(layout)
        self.keys = jnp.concatenate([b[:, :HEAD_SIZE] for b in refs[:count]], axis=0)
        self.values = jnp.concatenate([b[:, HEAD_SIZE:] for b in refs[:count]], axis=0)
        self.refs = refs[count:]
        self.bias = [bias(place, self.rows, ids, tree) for bias, place in layout]

    def blocks(self, x):
        return [x[i * self.rows : (i + 1) * self.rows] for i in range(len(self.bias))]

    def scores(self):
        out = []
        for x, bias in zip(self.blocks(dot_nt(self.keys, self.q)), self.bias):
            out.append(x if bias.shape[0] == 1 else x + per_head(bias))
        return out

    def dprobs(self):
        return self.blocks(dot_nt(self.values, self.ct))

    def top(self, scores):
        tops = []
        for x, bias in zip(scores, self.bias):
            top = jnp.max(x, axis=0, keepdims=True)
            tops.append(top + per_head(bias) if bias.shape[0] == 1 else top)
        return functools.reduce(jnp.maximum, tops)

    def weights(self, scores, top):
        out = []
        for x, bias in zip(scores, self.bias):
            row = top - per_head(bias) if bias.shape[0] == 1 else top
            out.append(jnp.exp2((x - row) * EXP2_SCALE))
        return out


def column_sum(parts):
    return functools.reduce(jnp.add, [jnp.sum(x, axis=0, keepdims=True) for x in parts])


def put_stats(stats, top, total, delta):
    stats[0, 0:1, :] = top
    stats[0, 1:2, :] = total
    stats[0, 2:3, :] = delta


def put_terms(out, dscore, probs, k):
    out[:, :HEAD_SIZE] = (dot_nn(dscore, k.q) * SCALE).astype(out.dtype)
    out[:, HEAD_SIZE:] = dot_nn(probs, k.ct).astype(out.dtype)


def rounded(parts):
    return jnp.concatenate([x.astype(jnp.bfloat16) for x in parts], axis=0)


def put_rows(x, mine, sibling, rows):
    for g in range(GROUP):
        columns = slice(g * HEAD_SIZE, (g + 1) * HEAD_SIZE)
        for i, out in enumerate((mine, sibling)):
            part = slice((2 * g + i) * rows, (2 * g + i + 1) * rows)
            out[:, columns] = x[:, part].T.astype(out.dtype)


def forward_kernel(layout, ids, tree, qm, qs, cm, cs, *refs):
    k = Keys(layout, ids, tree, qm, qs, cm, cs, refs)
    stats, terms, att_t = k.refs
    scores = k.scores()
    top = k.top(scores)
    e = k.weights(scores, top)
    inverse = 1.0 / column_sum(e)
    probs = [x * inverse for x in e]
    all_rounded = rounded(probs)
    att = dot_nn(k.values.T, all_rounded).astype(jnp.bfloat16)
    att_t[0] = att
    att = att.astype(jnp.float32)
    delta = jnp.sum(att * k.ct.T.astype(jnp.float32), axis=0, keepdims=True)
    put_stats(stats, top, inverse, delta)
    last = terms.shape[0] // k.rows
    dprobs = dot_nt(k.values[-terms.shape[0] :], k.ct)
    dprobs = [dprobs[i * k.rows : (i + 1) * k.rows] for i in range(last)]
    dscore = rounded([p * (d - delta) for p, d in zip(probs[-last:], dprobs)])
    put_terms(terms, dscore, all_rounded[-terms.shape[0] :], k)


def probs_dscore(k, stats):
    inverse, delta = stats[0, 1:2, :], stats[0, 2:3, :]
    probs = [x * inverse for x in k.weights(k.scores(), stats[0, 0:1, :])]
    dscore = [p * (d - delta) for p, d in zip(probs, k.dprobs())]
    return rounded(probs), rounded(dscore)


def terms_kernel(layout, ids, tree, qm, qs, cm, cs, *refs):
    k = Keys(layout, ids, tree, qm, qs, cm, cs, refs)
    stats, terms = k.refs
    probs, dscore = probs_dscore(k, stats)
    put_terms(terms, dscore, probs, k)


def rows_kernel(layout, ids, tree, qm, qs, cm, cs, *refs):
    k = Keys(layout, ids, tree, qm, qs, cm, cs, refs)
    stats, att_t, _, att_m, att_s, dq_m, dq_s, near, far, token = k.refs
    token[...] = jnp.zeros_like(token)
    rows = k.rows
    probs, dscore = probs_dscore(k, stats)
    half = near.shape[0]
    put_terms(near, dscore[:half], probs[:half], k)
    put_terms(far, dscore[half : 2 * half], probs[half : 2 * half], k)
    put_rows(att_t[0], att_m, att_s, rows)
    put_rows(dot_nn(k.keys.T, dscore) * SCALE, dq_m, dq_s, rows)


def halves_kernel(side, q, c, q_mine, q_other, c_mine, c_other, done):
    width = q_mine.shape[1]
    copies = []
    for x, out, place in (
        (q, q_other, 1 - side[0]),
        (c, c_other, 1 - side[0]),
        (q, q_mine, side[0]),
        (c, c_mine, side[0]),
    ):
        part = pl.ds(pl.multiple_of(place * width, HEAD_SIZE), width)
        copies.append(pltpu.make_async_copy(x.at[:, part], out, done.at[len(copies)]))
    for copy in copies:
        copy.start()
    for copy in copies:
        copy.wait()


def halves(side, q, c):
    half = jax.ShapeDtypeStruct((q.shape[0], q.shape[1] // 2), q.dtype)
    hbm = pl.BlockSpec(memory_space=pltpu.MemorySpace.HBM)
    return pl.pallas_call(
        halves_kernel,
        in_specs=[pl.BlockSpec(memory_space=pltpu.SMEM), hbm, hbm],
        out_specs=[pl.BlockSpec(memory_space=pltpu.VMEM)] * 4,
        out_shape=[half] * 4,
        scratch_shapes=[pltpu.SemaphoreType.DMA((4,))],
        cost_estimate=pl.CostEstimate(flops=0, bytes_accessed=8 * q.size, transcendentals=0),
    )(side.astype(jnp.int32).reshape(1), q, c)


def call(kernel, layout, heads, scalars, work, blocks, inputs, outs, products, tie=None):
    rows = work[0].shape[0]
    first, count = heads
    ins = [*work, *blocks, *inputs]
    if tie is not None:
        ins.append(tie)
        outs = [*outs, jax.ShapeDtypeStruct(tie.shape, tie.dtype)]

    def part(ref, j, held):
        if len(ref.shape) == 3:
            return ref.at[j : j + 1]
        width = ref.shape[1] // held
        return ref.at[:, j * width : (j + 1) * width]

    def body(ids, tree, *refs):
        given, made = refs[: len(ins)], refs[len(ins) :]
        for i in range(count):
            views = [part(r, first + i, HEADS) for r in given] + [part(r, i, count) for r in made]
            if tie is not None:
                views[len(ins) - 1], views[-1] = given[-1], made[-1]
            kernel(layout, ids, tree, *views)

    vmem = pl.BlockSpec(memory_space=pltpu.VMEM)
    smem = pl.BlockSpec(memory_space=pltpu.SMEM)
    specs = [smem, smem, *[vmem] * len(ins)]
    if tie is not None:
        specs[-1] = pl.BlockSpec(memory_space=pl.ANY)
    flops = count * 2 * products * (2 * rows * GROUP) * (len(blocks) * rows) * HEAD_SIZE
    return pl.pallas_call(
        body,
        in_specs=specs,
        out_specs=[vmem] * len(outs),
        out_shape=outs,
        compiler_params=pltpu.CompilerParams(vmem_limit_bytes=VMEM_BYTES),
        cost_estimate=pl.CostEstimate(
            flops=flops, bytes_accessed=count * 4 * 2 * rows * WIDTH * 2, transcendentals=0
        ),
    )(*scalars, *ins)


def after(x, *tokens):
    return lax.optimization_barrier((x, *tokens))[0]


def on_device(seq_count, head_count, queries, rotated_key_rows, value_matrix, cotangent, tree_mask):
    s = lax.axis_index("seq")
    h = lax.axis_index("head")
    rows = queries.shape[0]
    core = h & 1
    scalars = (jnp.stack([h, s]).astype(jnp.int32), tree_mask)
    f32, bf16 = jnp.float32, jnp.bfloat16
    shape = jax.ShapeDtypeStruct

    def send(x, mask):
        return lax.ppermute(x, "head", [(i, i ^ mask) for i in range(head_count)])

    def columns(x, place, width):
        return lax.dynamic_slice_in_dim(x, place * width, width, 1)

    def half(kv, place):
        k, v = [columns(x, place, HEADS * HEAD_SIZE) for x in kv]
        parts = []
        for j in range(HEADS):
            part = slice(j * HEAD_SIZE, (j + 1) * HEAD_SIZE)
            parts += [k[:, part], v[:, part]]
        return jnp.concatenate(parts, axis=1)

    def gathered(kv, place):
        mine, other = half(kv, place), half(kv, 1 - place)
        return [mine, send(other, 1), send(mine, 2), send(other, 3)]

    hops = [1]
    step = seq_count // 2
    while step > 1:
        hops.append(step)
        step //= 2
    held = (rotated_key_rows, value_matrix)
    for hop, step in enumerate(hops):
        reached = seq_count if hop == 0 else 2 * step
        sends = [(i, i + step) for i in range(0, seq_count, reached)]
        if hop:
            sends += [(i + 1, i + 1 + step) for i, _ in sends]
            place = s - s % 2
            got = lax.ppermute(held, "seq", sends)
        else:
            place = s
            got = jnp.concatenate([lax.ppermute(x, "seq", sends) for x in held], axis=1)
            held = lax.optimization_barrier(jnp.concatenate(held, axis=1))
        held = jnp.where(place % reached == step, got, held)
        if hop == 0:
            side = after(core, held[:16, :HEAD_SIZE])
            own_blocks = gathered((rotated_key_rows, value_matrix), side)
            q_mine, q_other, c_mine, c_other = halves(side, queries, cotangent)
            q_sib, c_sib = send(q_other, 1), send(c_other, 1)
        if hop == 1:
            held, q_mine, q_sib, c_sib = lax.optimization_barrier((held, q_mine, q_sib, c_sib))
    width = KEY_VALUE_HEADS * HEAD_SIZE
    prompt = (held[:, :width], held[:, width:])
    work = (q_mine, q_sib, c_mine, c_sib)
    prompt_blocks = gathered(prompt, core)

    near, far = (0, 1), (2, 3)
    own_all = tuple((own_bias, b) for b in near + far)
    every, one = (0, HEADS), 1

    def stats_shape():
        return shape((HEADS, 8, 2 * GROUP * rows), f32)

    def terms_shape(count, dtype):
        return shape((2 * rows, 2 * count * HEAD_SIZE), dtype)

    layout = own_all + tuple((prompt_bias, b) for b in near + far)
    blocks = [*own_blocks, *prompt_blocks]
    att_shape = shape((HEADS, HEAD_SIZE, 2 * GROUP * rows), bf16)
    outs = [stats_shape(), terms_shape(HEADS, bf16), att_shape]
    stats, terms_far, att_t = call(
        forward_kernel, layout, every, scalars, work, blocks, [], outs, 5
    )
    layout = tuple((prompt_bias, b) for b in near)
    outs = [terms_shape(HEADS, bf16)]
    terms = call(
        terms_kernel, layout, every, scalars, work, prompt_blocks[:2], [stats], outs, 4
    )[0]

    def plus(a, b):
        return a.astype(f32) + b.astype(f32)

    def across(x, pairs):
        flat = []
        for h in range(head_count):
            flat += [(a * head_count + h, b * head_count + (h ^ mask)) for a, b, mask in pairs]
        return lax.ppermute(x, ("seq", "head"), flat)

    even = range(0, seq_count, 2)
    got_far = across(terms_far, [(i, i, 2) for i in even])
    got_next_far = across(terms_far, [(i + 1, i, 2) for i in even])
    got_next = across(terms, [(i + 1, i, 0) for i in even])
    layout = own_all + tuple((prompt_bias, b) for b in near + far)
    blocks = [*own_blocks, *prompt_blocks]
    att, dq, own_sums = [], [], []
    total, tie = None, terms
    step, hop = 1, 0
    while step < seq_count:
        if hop:
            got = lax.ppermute(total, "seq", [(i + step, i) for i in range(0, seq_count, 2 * step)])
        if hop < HEADS:
            outs = [shape((rows, WIDTH), bf16)] * 4 + [terms_shape(1, f32), terms_shape(1, bf16)]
            a_m, a_s, d_m, d_s, own_near, own_far, token = call(
                rows_kernel, layout, (hop, one), scalars, work, blocks, [stats, att_t], outs, 8, tie
            )
            att.append((a_m, send(a_s, 1)))
            dq.append((d_m, send(d_s, 1)))
            own_sums.append((own_near, own_far))
        else:
            token = jnp.zeros_like(total)
        if hop:
            total = total + (got + token)
        else:
            total = plus(plus(terms, got_far), plus(got_next_far, got_next)) + token.astype(f32)
            total = total.astype(bf16)
        tie = total
        step *= 2
        hop += 1

    def both_halves(parts):
        mine = jnp.concatenate([x for x, _ in parts], axis=1)
        theirs = jnp.concatenate([x for _, x in parts], axis=1)
        return jnp.where(
            core == 0,
            jnp.concatenate([mine, theirs], axis=1),
            jnp.concatenate([theirs, mine], axis=1),
        )

    attention, query_grad = both_halves(att), both_halves(dq)
    total = jnp.where(s == 0, total.astype(f32), jnp.float32(0.0))
    own_near, own_far = [jnp.concatenate(x, axis=1) for x in zip(*own_sums)]
    total = (plus(own_near, send(own_far, 2)) + total).astype(bf16)
    total = both_halves([(total[:rows], send(total[rows:], 1))])

    def gradient(first):
        parts = []
        for j in range(KEY_VALUE_HEADS):
            start = (2 * j + first) * HEAD_SIZE
            parts.append(total[:, start : start + HEAD_SIZE])
        return jnp.concatenate(parts, axis=1)

    return (attention, query_grad, gradient(0), gradient(1))


def solution(mesh):
    spec = P(("seq", "head"), None)
    return jax.shard_map(
        functools.partial(on_device, mesh.shape["seq"], mesh.shape["head"]),
        mesh=mesh,
        in_specs=(spec, spec, spec, spec, P("seq", None)),
        out_specs=(spec, spec, spec, spec),
        check_vma=False,
    )
```
